256 devices in a mesh: wide: 16 (over z, y_hi), narrow: 16 (over y_lo, x, core).
Axes of the slice: x: 4, y: 4 (y_hi: 2, y_lo: 2; y = y_hi * 2 + y_lo), z: 8, core: 2. Of those that a mesh axis runs over, the one named last changes fastest.
Arguments:
- sources: bfloat16 [16384, 1024], P('narrow'), may hold values from -16 to 16
- targets: bfloat16 [32768, 1024], P(('wide', 'narrow')), may hold values from -16 to 16
Outputs:
- row_best: float32 [16384], P('narrow')
- col_best: float32 [32768], P(('wide', 'narrow'))
The draws below stay inside these ranges and needn't reach their ends.
All inputs are finite; a program needn't handle non-finite values.
Results may differ from the reference program's by a relative error of at most 0.0003.
Values may be sent and summed in bfloat16 or wider, within the bound.
No kernel may reach another device: no remote copies, remote signals or barrier semaphores. Data moves between devices by JAX's collectives and lax.ppermute only.
A program may use at most 64 MiB of HBM per device.

```python
import math
import jax
import jax.numpy as jnp
from jax import lax

D = 1024
SOURCES = 16384
TARGETS = 32768


def shared_vectors(key):
    return jax.random.truncated_normal(key, -2.5, 2.5, (8, D), jnp.float32)


def drawn_strength(count):
    target_score = 140.0 + 20.0 * jnp.arange(count, dtype=jnp.float32)
    return jnp.sqrt(target_score / jnp.sqrt(jnp.float32(D)))


def draw_sources(key, part):
    shared = shared_vectors(key)
    key = jax.random.fold_in(key, 11)
    values = jax.random.truncated_normal(key, -4.0, 4.0, (SOURCES, D), jnp.float32)
    strength = drawn_strength(8)
    chosen_rows = jnp.arange(8, dtype=jnp.int32) * (SOURCES // 8)
    values = values.at[chosen_rows].set(shared * strength[:, None])
    return values.astype(jnp.bfloat16)


def draw_targets(key, part):
    shared = shared_vectors(key)
    key = jax.random.fold_in(key, 23)
    values = jax.random.truncated_normal(key, -4.0, 4.0, (TARGETS, D), jnp.float32)
    strength = drawn_strength(8)
    shrink = 2.0 / (strength * strength * jnp.sqrt(jnp.float32(D)))
    jitter = 0.05 * jax.random.truncated_normal(jax.random.fold_in(key, 3), -4.0, 4.0, (8, D), jnp.float32)
    chosen_rows = jnp.arange(8, dtype=jnp.int32) * (TARGETS // 8)
    values = values.at[chosen_rows].set(shared * strength[:, None])
    values = values.at[chosen_rows + 1].set(shared * (strength * (1.0 - shrink))[:, None] + jitter)
    return values.astype(jnp.bfloat16)


def setup_inputs(seed: int = 0) -> dict:
    arg_keys = jax.random.split(jax.random.key(seed), 3)
    return {
        "sources": draw_sources(jax.random.fold_in(arg_keys[2], 71), 0),
        "targets": draw_targets(jax.random.fold_in(arg_keys[2], 71), 0),
    }


def reference(sources, targets):
    inverse_root = 1.0 / math.sqrt(D)
    tile_rows = 512 if SOURCES % 512 == 0 else SOURCES
    source_tiles = sources.reshape(SOURCES // tile_rows, tile_rows, D)

    def score_tile(source_tile):
        return jnp.dot(source_tile, targets.T, preferred_element_type=jnp.float32) * inverse_root

    def first_pass(running, source_tile):
        col_max, col_sum = running
        scores = score_tile(source_tile)
        row_max = lax.optimization_barrier(jnp.max(scores, axis=1))
        row_norm = row_max + jnp.log(lax.optimization_barrier(jnp.sum(jnp.exp(scores - row_max[:, None]), axis=1)))
        tile_max = lax.optimization_barrier(jnp.max(scores, axis=0))
        joint_max = jnp.maximum(col_max, tile_max)
        tile_sum = lax.optimization_barrier(jnp.sum(jnp.exp(scores - tile_max[None, :]), axis=0))
        joint_sum = col_sum * jnp.exp(col_max - joint_max) + tile_sum * jnp.exp(tile_max - joint_max)
        return ((joint_max, joint_sum), row_norm)
    initial = (jnp.full((TARGETS,), -1e+30, jnp.float32), jnp.zeros((TARGETS,), jnp.float32))
    (col_max, col_sum), row_norms = lax.scan(first_pass, initial, source_tiles)
    col_norm = col_max + jnp.log(col_sum)

    def second_pass(col_best, inputs):
        source_tile, tile_norm = inputs
        margins = score_tile(source_tile) - 0.5 * (tile_norm[:, None] + col_norm[None, :])
        return (jnp.maximum(col_best, lax.optimization_barrier(jnp.max(margins, axis=0))), lax.optimization_barrier(jnp.max(margins, axis=1)))
    col_best, row_best = lax.scan(second_pass, jnp.full((TARGETS,), -1e+30, jnp.float32), (source_tiles, row_norms))
    return (row_best.reshape(SOURCES), col_best)
```

```python
import functools
import math

import jax
import jax.numpy as jnp
from jax import lax
from jax.experimental import pallas as pl
from jax.experimental.pallas import tpu as pltpu
from jax.sharding import PartitionSpec as P

XS, YS, ZS, CORES = 4, 4, 8, 2
BOTH = ("wide", "narrow")
GROUP = 8
LANES = 128


def device_index(z, y, x, core):
    y, x, z = y % YS, x % XS, z % ZS
    return (z * 2 + y // 2) * 16 + (y % 2) * 8 + x * 2 + core


def places():
    for z in range(ZS):
        for y in range(YS):
            for x in range(XS):
                for core in range(CORES):
                    yield z, y, x, core


def partner(y, core):
    return y ^ 1 if core == 0 else 3 - y


def move(value, where):
    pairs = [(device_index(*place), device_index(*where(*place))) for place in places()]
    return lax.ppermute(value, BOTH, pairs)


to_core = lambda z, y, x, core: (z, y, x, 1 - core)
to_right = lambda z, y, x, core: (z, y, x + 1, core)
to_left = lambda z, y, x, core: (z, y, x - 1, core)
to_far = lambda z, y, x, core: (z, y, x + 2, core)
to_partner = lambda z, y, x, core: (z, partner(y, core), x, core)


def column_groups():
    groups = []
    for z in range(ZS):
        for core in range(CORES):
            for y in (0, 2):
                rows = (y, partner(y, core))
                groups.append([device_index(z, row, x, core) for row in rows for x in range(XS)])
    return groups


def vmem():
    return pl.BlockSpec(memory_space=pltpu.VMEM)


def held(value):
    return pltpu.with_memory_space_constraint(value, pltpu.VMEM)


def call(kernel, out_shape, *operands, flops=0, exps=0, scratch=(), limit=24):
    moved = sum(math.prod(o.shape) * o.dtype.itemsize for o in operands)
    return pl.pallas_call(
        kernel,
        out_shape=out_shape,
        in_specs=[vmem() for _ in operands],
        out_specs=jax.tree.map(lambda _: vmem(), out_shape),
        scratch_shapes=list(scratch),
        cost_estimate=pl.CostEstimate(flops=flops, bytes_accessed=moved, transcendentals=exps),
        compiler_params=pltpu.CompilerParams(vmem_limit_bytes=limit * 1024 * 1024),
    )(*operands)


def f32(*shape):
    return jax.ShapeDtypeStruct(shape, jnp.float32)


def eye():
    row = lax.broadcasted_iota(jnp.int32, (LANES, LANES), 0)
    return row == lax.broadcasted_iota(jnp.int32, (LANES, LANES), 1)


def as_row(column):
    return jnp.sum(jnp.where(eye(), column, 0.0), axis=0, keepdims=True)


def as_column(row):
    return jnp.sum(jnp.where(eye(), row, 0.0), axis=1, keepdims=True)


def own_place():
    narrow = lax.axis_index("narrow")
    return narrow // 8, (narrow // 2) % 4


def owner(place, slot):
    y_lo, x = place
    dx, dy = slot
    return ((y_lo + dy) % 2) * 4 + (x + dx) % 4


SLOTS = ((0, 0), (0, 1), (3, 0), (1, 0), (3, 1), (1, 1), (2, 0), (2, 1))


def first_kernel(scale, s0, s1, ta, tb, scores, row_part, col_part):
    rate = scale / math.log(2.0)
    targets = jnp.concatenate([ta[...], tb[...]], axis=0)
    running = None
    for i in range(8):
        source = (s0 if i < 4 else s1)[pl.ds((i % 4) * 256, 256), :]
        part = lax.dot_general(
            targets, source, (((1,), (1,)), ((), ())), preferred_element_type=jnp.float32
        )
        scores[:, pl.ds(i * 256, 256)] = part
        top = jnp.max(part, axis=0, keepdims=True)
        total = jnp.sum(jnp.exp2((part - top) * rate), axis=0, keepdims=True)
        result = top * scale + jnp.log(total)
        row_part[pl.ds(2 * i, 1), :] = result[:, :LANES]
        row_part[pl.ds(2 * i + 1, 1), :] = result[:, LANES:]
        top = jnp.maximum(part[:, :LANES], part[:, LANES:])
        running = top if running is None else jnp.maximum(running, top)
    top = jnp.max(running, axis=1, keepdims=True)
    total = jnp.zeros((256, LANES), jnp.float32)
    for j in range(16):
        total += jnp.exp2((scores[:, pl.ds(j * LANES, LANES)] - top) * rate)
    result = top * scale + jnp.log(jnp.sum(total, axis=1, keepdims=True))
    col_part[pl.ds(0, 1), :] = as_row(result[:LANES])
    col_part[pl.ds(1, 1), :] = as_row(result[LANES:])


def log_sum(parts):
    top = functools.reduce(jnp.maximum, parts)
    return top + jnp.log(sum(jnp.exp(part - top) for part in parts))


def pack_kernel(r0, r1, r2, r3, c0, c1, c2, c3, row_own, row_other, sent, scratch):
    parts = [r0[...], r1[...], r2[...], r3[...]]
    joint = log_sum(parts)
    row_own[...] = joint[:8]
    row_other[...] = joint[8:]
    place = own_place()
    for k, slot in enumerate(SLOTS):
        source = (c0, c1, c2, c3)[k // 2]
        scratch[pl.ds(owner(place, slot), 1), :] = source[pl.ds(k % 2, 1), :]
    whole = scratch[...]
    for e in range(GROUP):
        sent[pl.ds(e * GROUP, GROUP), :] = whole


def row_best_kernel(scale, a0, a1, a2, a3, received, best_own, best_other, col_norm):
    norm = log_sum([received[pl.ds(e * GROUP, GROUP), :] for e in range(GROUP)])
    col_norm[...] = norm
    place = own_place()
    half = 0.5 / scale
    best = [None] * 16
    for k, slot in enumerate(SLOTS):
        column = as_column(col_norm[pl.ds(owner(place, slot), 1), :]) * half
        column = jnp.broadcast_to(column, (LANES, LANES))
        block = (a0, a1, a2, a3)[k // 2]
        for j in range(16):
            part = block[pl.ds((k % 2) * LANES, LANES), pl.ds(j * LANES, LANES)] - column
            part = functools.reduce(jnp.maximum, [part[8 * q : 8 * q + 8] for q in range(16)])
            best[j] = part if k == 0 else jnp.maximum(best[j], part)
    for j in range(16):
        out = best_own if j < 8 else best_other
        out[pl.ds(j % 8, 1), :] = jnp.max(best[j], axis=0, keepdims=True) * scale


def join_kernel(row_own, row_in, best_own, best_in, sent):
    norm = log_sum([row_own[...], row_in[...]])
    best = jnp.maximum(best_own[...], best_in[...])
    for e in range(16):
        sent[pl.ds(e * 16, 8), :] = norm
        sent[pl.ds(e * 16 + 8, 8), :] = best


def row_norm_kernel(received, row_norm, row_best):
    norm = log_sum([received[pl.ds(e * 16, 8), :] for e in range(16)])
    best = functools.reduce(jnp.maximum, [received[pl.ds(e * 16 + 8, 8), :] for e in range(16)])
    row_norm[...] = norm
    row_best[...] = best - 0.5 * norm


def col_best_kernel(scale, a0, a1, a2, a3, norm_own, norm_other, sent):
    place = own_place()
    half = 0.5 / scale
    own, other = norm_own[...] * half, norm_other[...] * half
    for k, slot in enumerate(SLOTS):
        block = (a0, a1, a2, a3)[k // 2]
        best = None
        for j in range(16):
            norm = (own if j < 8 else other)[j % 8 : j % 8 + 1, :]
            part = block[pl.ds((k % 2) * LANES, LANES), pl.ds(j * LANES, LANES)] - norm
            best = part if best is None else jnp.maximum(best, part)
        best = as_row(jnp.max(best, axis=1, keepdims=True)) * scale
        sent[pl.ds(owner(place, slot), 1), :] = best


def last_kernel(received, col_norm, col_best):
    y_lo, x = own_place()
    best = jnp.max(received[...], axis=0, keepdims=True)
    col_best[...] = best - 0.5 * col_norm[pl.ds(y_lo * 4 + x, 1), :]


def body(sources, targets):
    scale = 1.0 / math.sqrt(sources.shape[1])
    groups = column_groups()

    def exchange(value):
        return lax.all_to_all(value, BOTH, 0, 0, axis_index_groups=groups, tiled=True)

    other_sources = held(move(sources, to_core))
    sources = held(sources)
    blocks = {(0, 0): targets}
    blocks[3, 0] = move(targets, to_right)
    blocks[1, 0] = move(targets, to_left)
    blocks[2, 0] = move(targets, to_far)
    for dx in range(4):
        blocks[dx, 1] = move(blocks[dx, 0], to_partner)

    scores, rows, cols = [], [], []
    for k in range(0, GROUP, 2):
        part, row, col = call(
            functools.partial(first_kernel, scale),
            (pltpu.VMEM((256, 2048), jnp.float32), f32(16, LANES), f32(2, LANES)),
            sources,
            other_sources,
            blocks[SLOTS[k]],
            blocks[SLOTS[k + 1]],
            flops=2 * 256 * 2048 * 1024,
            exps=2 * 256 * 2048,
        )
        scores.append(held(part))
        rows.append(row)
        cols.append(col)
    row_own, row_other, sent = call(
        pack_kernel,
        (f32(8, LANES), f32(8, LANES), f32(GROUP * GROUP, LANES)),
        *rows,
        *cols,
        scratch=[pltpu.VMEM((GROUP, LANES), jnp.float32)],
    )
    row_in = move(row_other, to_core)
    received = exchange(sent)
    best_own, best_other, col_norm = call(
        functools.partial(row_best_kernel, scale),
        (f32(8, LANES), f32(8, LANES), f32(GROUP, LANES)),
        *scores,
        received,
        flops=2 * 1024 * 2048,
    )
    best_in = move(best_other, to_core)
    sent = call(join_kernel, f32(256, LANES), row_own, row_in, best_own, best_in)
    received = lax.all_to_all(sent, "wide", 0, 0, tiled=True)
    row_norm, row_best = call(row_norm_kernel, (f32(8, LANES), f32(8, LANES)), received)
    other_norm = move(row_norm, to_core)
    sent = call(
        functools.partial(col_best_kernel, scale),
        f32(GROUP, LANES),
        *scores,
        row_norm,
        other_norm,
        flops=2 * 1024 * 2048,
    )
    received = exchange(sent)
    col_best = call(last_kernel, f32(1, LANES), received, col_norm)
    return row_best.reshape(1024), col_best.reshape(LANES)


def solution(mesh):
    return jax.shard_map(
        body,
        mesh=mesh,
        in_specs=(P("narrow", None), P(("wide", "narrow"), None)),
        out_specs=(P("narrow"), P(("wide", "narrow"))),
        check_vma=False,
    )
```

```python
import functools
import math

import jax
import jax.numpy as jnp
from jax import lax
from jax.experimental import pallas as pl
from jax.experimental.pallas import tpu as pltpu
from jax.sharding import PartitionSpec as P

XS, YS, ZS, CORES = 4, 4, 8, 2
BOTH = ("wide", "narrow")
GROUP = 8
LANES = 128


def device_index(z, y, x, core):
    y, x, z = y % YS, x % XS, z % ZS
    return (z * 2 + y // 2) * 16 + (y % 2) * 8 + x * 2 + core


def places():
    for z in range(ZS):
        for y in range(YS):
            for x in range(XS):
                for core in range(CORES):
                    yield z, y, x, core


def partner(y, core):
    return y ^ 1 if core == 0 else 3 - y


def move(value, where):
    pairs = [(device_index(*place), device_index(*where(*place))) for place in places()]
    return lax.ppermute(value, BOTH, pairs)


def ahead(z, y, x, core):
    return z, y, x + 1 - 2 * core, core


def behind(z, y, x, core):
    return z, y, x - 1 + 2 * core, core


def across(z, y, x, core):
    return z, partner(y, core), x, core


def to_core(z, y, x, core):
    return z, y, x, 1 - core


def column_groups():
    groups = []
    for z in range(ZS):
        for core in range(CORES):
            for y in (0, 2):
                rows = (y, partner(y, core))
                groups.append([device_index(z, row, x, core) for row in rows for x in range(XS)])
    return groups


def vmem():
    return pl.BlockSpec(memory_space=pltpu.VMEM)


def held(value):
    return pltpu.with_memory_space_constraint(value, pltpu.VMEM)


def call(kernel, out_shape, *operands, flops=0, exps=0, scratch=(), limit=24):
    moved = sum(math.prod(o.shape) * o.dtype.itemsize for o in operands)
    return pl.pallas_call(
        kernel,
        out_shape=out_shape,
        in_specs=[vmem() for _ in operands],
        out_specs=jax.tree.map(lambda _: vmem(), out_shape),
        scratch_shapes=list(scratch),
        cost_estimate=pl.CostEstimate(flops=flops, bytes_accessed=moved, transcendentals=exps),
        compiler_params=pltpu.CompilerParams(vmem_limit_bytes=limit * 1024 * 1024),
    )(*operands)


def f32(*shape):
    return jax.ShapeDtypeStruct(shape, jnp.float32)


def eye():
    row = lax.broadcasted_iota(jnp.int32, (LANES, LANES), 0)
    return row == lax.broadcasted_iota(jnp.int32, (LANES, LANES), 1)


def as_row(column):
    return jnp.sum(jnp.where(eye(), column, 0.0), axis=0, keepdims=True)


def as_column(row):
    return jnp.sum(jnp.where(eye(), row, 0.0), axis=1, keepdims=True)


def own_place():
    narrow = lax.axis_index("narrow")
    return narrow // 8, (narrow // 2) % 4, narrow % 2


def owner(place, slot):
    y_lo, x, core = place
    dx, dy = slot
    return ((y_lo + dy) % 2) * 4 + (x + 4 + dx * (1 - 2 * core)) % 4


CALLS = (((0, 0), (0, 1)), ((3, 0), (1, 0)), ((3, 1), (1, 1)), ((2, 0),), ((2, 1),))
SLOTS = tuple((call, k, slot) for call, slots in enumerate(CALLS) for k, slot in enumerate(slots))


def products(scale, s0, s1, targets, scores, row_part):
    count = targets.shape[0]
    rate = scale / math.log(2.0)
    running = None
    for i in range(8):
        source = (s0 if i < 4 else s1)[pl.ds((i % 4) * 256, 256), :]
        part = lax.dot_general(
            targets, source, (((1,), (1,)), ((), ())), preferred_element_type=jnp.float32
        )
        scores[:, pl.ds(i * 256, 256)] = part
        top = jnp.max(part, axis=0, keepdims=True)
        total = jnp.sum(jnp.exp2((part - top) * rate), axis=0, keepdims=True)
        result = top * scale + jnp.log(total)
        row_part[pl.ds(2 * i, 1), :] = result[:, :LANES]
        row_part[pl.ds(2 * i + 1, 1), :] = result[:, LANES:]
        top = jnp.maximum(part[:, :LANES], part[:, LANES:])
        running = top if running is None else jnp.maximum(running, top)
    top = jnp.max(running, axis=1, keepdims=True)
    total = jnp.zeros((count, LANES), jnp.float32)
    for j in range(16):
        total += jnp.exp2((scores[:, pl.ds(j * LANES, LANES)] - top) * rate)
    result = top * scale + jnp.log(jnp.sum(total, axis=1, keepdims=True))
    return [as_row(result[k : k + LANES]) for k in range(0, count, LANES)]


def pair_kernel(scale, s0, s1, ta, tb, scores, row_part, col_part):
    targets = jnp.concatenate([ta[...], tb[...]], axis=0)
    for k, row in enumerate(products(scale, s0, s1, targets, scores, row_part)):
        col_part[pl.ds(k, 1), :] = row


def single_kernel(scale, s0, s1, ta, scores, row_part, col_part):
    col_part[...] = products(scale, s0, s1, ta[...], scores, row_part)[0]


def end_kernel(scale, s0, s1, ta, *refs):
    rows, cols = refs[:4], refs[4:8]
    scores, joint, sent, scratch, last = refs[8:]
    (col,) = products(scale, s0, s1, ta[...], scores, last)
    joint[...] = log_sum([row[...] for row in rows] + [last[...]])
    place = own_place()
    for call, k, slot in SLOTS:
        row = col if call == 4 else cols[call][pl.ds(k, 1), :]
        scratch[pl.ds(owner(place, slot), 1), :] = row
    whole = scratch[...]
    for e in range(GROUP):
        sent[pl.ds(e * GROUP, GROUP), :] = whole


def log_sum(parts):
    top = functools.reduce(jnp.maximum, parts)
    return top + jnp.log(sum(jnp.exp(part - top) for part in parts))


def row_best_kernel(scale, a0, a1, a2, a3, a4, received, row_joint, own, other, col_norm):
    norm = log_sum([received[pl.ds(e * GROUP, GROUP), :] for e in range(GROUP)])
    col_norm[...] = norm
    place = own_place()
    half = 0.5 / scale
    best = [None] * 16
    for call, k, slot in SLOTS:
        column = as_column(col_norm[pl.ds(owner(place, slot), 1), :]) * half
        column = jnp.broadcast_to(column, (LANES, LANES))
        block = (a0, a1, a2, a3, a4)[call]
        for j in range(16):
            part = block[pl.ds(k * LANES, LANES), pl.ds(j * LANES, LANES)] - column
            part = functools.reduce(jnp.maximum, [part[8 * q : 8 * q + 8] for q in range(16)])
            best[j] = part if best[j] is None else jnp.maximum(best[j], part)
    for j in range(16):
        out = own if j < 8 else other
        out[pl.ds(8 + j % 8, 1), :] = jnp.max(best[j], axis=0, keepdims=True) * scale
    own[:8] = row_joint[:8]
    other[:8] = row_joint[8:]


def join_kernel(own, incoming, sent):
    norm = log_sum([own[:8], incoming[:8]])
    best = jnp.maximum(own[8:], incoming[8:])
    for e in range(16):
        sent[pl.ds(e * 16, 8), :] = norm
        sent[pl.ds(e * 16 + 8, 8), :] = best


def row_norm_kernel(received, row_norm, row_best):
    norm = log_sum([received[pl.ds(e * 16, 8), :] for e in range(16)])
    best = functools.reduce(jnp.maximum, [received[pl.ds(e * 16 + 8, 8), :] for e in range(16)])
    row_norm[...] = norm
    row_best[...] = best - 0.5 * norm


def col_best_kernel(scale, a0, a1, a2, a3, a4, norm_own, norm_other, sent):
    place = own_place()
    half = 0.5 / scale
    own, other = norm_own[...] * half, norm_other[...] * half
    for call, k, slot in SLOTS:
        block = (a0, a1, a2, a3, a4)[call]
        best = None
        for j in range(16):
            norm = (own if j < 8 else other)[j % 8 : j % 8 + 1, :]
            part = block[pl.ds(k * LANES, LANES), pl.ds(j * LANES, LANES)] - norm
            best = part if best is None else jnp.maximum(best, part)
        best = as_row(jnp.max(best, axis=1, keepdims=True)) * scale
        sent[pl.ds(owner(place, slot), 1), :] = best


def last_kernel(received, col_norm, col_best):
    y_lo, x, _ = own_place()
    best = jnp.max(received[...], axis=0, keepdims=True)
    col_best[...] = best - 0.5 * col_norm[pl.ds(y_lo * 4 + x, 1), :]


def body(sources, targets):
    scale = 1.0 / math.sqrt(sources.shape[1])
    groups = column_groups()

    def exchange(value):
        return lax.all_to_all(value, BOTH, 0, 0, axis_index_groups=groups, tiled=True)

    def kept(rows):
        return pltpu.VMEM((rows, 2048), jnp.float32)

    blocks = {(0, 0): targets}
    blocks[0, 1] = move(targets, across)
    blocks[3, 0] = move(targets, ahead)
    blocks[1, 0] = move(targets, behind)
    blocks[2, 0] = move(blocks[3, 0], ahead)
    for dx in (3, 1, 2):
        blocks[dx, 1] = move(blocks[dx, 0], across)
    both = (held(sources), held(move(sources, to_core)))

    scores, rows, cols = [], [], []
    for slots in CALLS[:-1]:
        count = len(slots) * LANES
        part, row, col = call(
            functools.partial(pair_kernel if len(slots) == 2 else single_kernel, scale),
            (kept(count), f32(16, LANES), f32(len(slots), LANES)),
            *both,
            *[blocks[slot] for slot in slots],
            flops=2 * count * 2048 * 1024,
            exps=2 * count * 2048,
        )
        scores.append(held(part))
        rows.append(row)
        cols.append(col)
    part, row_joint, sent = call(
        functools.partial(end_kernel, scale),
        (kept(LANES), f32(16, LANES), f32(GROUP * GROUP, LANES)),
        *both,
        blocks[CALLS[-1][0]],
        *rows,
        *cols,
        flops=2 * LANES * 2048 * 1024,
        exps=2 * LANES * 2048,
        scratch=[pltpu.VMEM((GROUP, LANES), jnp.float32), pltpu.VMEM((16, LANES), jnp.float32)],
    )
    scores.append(held(part))
    received = exchange(sent)
    own, other, col_norm = call(
        functools.partial(row_best_kernel, scale),
        (f32(16, LANES), f32(16, LANES), f32(GROUP, LANES)),
        *scores,
        received,
        row_joint,
        flops=2 * 1024 * 2048,
    )
    sent = call(join_kernel, f32(256, LANES), own, move(other, to_core))
    received = lax.all_to_all(sent, "wide", 0, 0, tiled=True)
    row_norm, row_best = call(row_norm_kernel, (f32(8, LANES), f32(8, LANES)), received)
    sent = call(
        functools.partial(col_best_kernel, scale),
        f32(GROUP, LANES),
        *scores,
        row_norm,
        move(row_norm, to_core),
        flops=2 * 1024 * 2048,
    )
    received = exchange(sent)
    col_best = call(last_kernel, f32(1, LANES), received, col_norm)
    return row_best.reshape(1024), col_best.reshape(LANES)


def solution(mesh):
    return jax.shard_map(
        body,
        mesh=mesh,
        in_specs=(P("narrow", None), P(("wide", "narrow"), None)),
        out_specs=(P("narrow"), P(("wide", "narrow"))),
        check_vma=False,
    )
```

```python
import functools
import math

import jax
import jax.numpy as jnp
from jax import lax
from jax.experimental import pallas as pl
from jax.experimental.pallas import tpu as pltpu
from jax.sharding import PartitionSpec as P

XS, YS, ZS, CORES = 4, 4, 8, 2
BOTH = ("wide", "narrow")
GROUP = 8
LANES = 128


def device_index(z, y, x, core):
    y, x, z = y % YS, x % XS, z % ZS
    return (z * 2 + y // 2) * 16 + (y % 2) * 8 + x * 2 + core


def places():
    for z in range(ZS):
        for y in range(YS):
            for x in range(XS):
                for core in range(CORES):
                    yield z, y, x, core


def partner(y, core):
    return y ^ 1 if core == 0 else 3 - y


def move(value, where):
    pairs = [(device_index(*place), device_index(*where(*place))) for place in places()]
    return lax.ppermute(value, BOTH, pairs)


def ahead(z, y, x, core):
    return z, y, x + 1 - 2 * core, core


def behind(z, y, x, core):
    return z, y, x - 1 + 2 * core, core


def across(z, y, x, core):
    return z, partner(y, core), x, core


def to_core(z, y, x, core):
    return z, y, x, 1 - core


def column_groups():
    groups = []
    for z in range(ZS):
        for core in range(CORES):
            for y in (0, 2):
                rows = (y, partner(y, core))
                groups.append([device_index(z, row, x, core) for row in rows for x in range(XS)])
    return groups


def vmem():
    return pl.BlockSpec(memory_space=pltpu.VMEM)


def after(values):
    return lax.optimization_barrier(values)


def held(value):
    return pltpu.with_memory_space_constraint(value, pltpu.VMEM)


def call(kernel, out_shape, *operands, flops=0, exps=0, scratch=(), far=(), limit=24):
    moved = sum(math.prod(o.shape) * o.dtype.itemsize for o in operands)
    return pl.pallas_call(
        kernel,
        out_shape=out_shape,
        in_specs=[pl.BlockSpec(memory_space=pltpu.HBM) if k in far else vmem() for k in range(len(operands))],
        out_specs=jax.tree.map(lambda _: vmem(), out_shape),
        scratch_shapes=list(scratch),
        cost_estimate=pl.CostEstimate(flops=flops, bytes_accessed=moved, transcendentals=exps),
        compiler_params=pltpu.CompilerParams(vmem_limit_bytes=limit * 1024 * 1024),
    )(*operands)


def f32(*shape):
    return jax.ShapeDtypeStruct(shape, jnp.float32)


def eye():
    row = lax.broadcasted_iota(jnp.int32, (LANES, LANES), 0)
    return row == lax.broadcasted_iota(jnp.int32, (LANES, LANES), 1)


def as_row(column):
    return jnp.sum(jnp.where(eye(), column, 0.0), axis=0, keepdims=True)


def as_column(row):
    return jnp.sum(jnp.where(eye(), row, 0.0), axis=1, keepdims=True)


def own_place():
    narrow = lax.axis_index("narrow")
    return narrow // 8, (narrow // 2) % 4, narrow % 2


def owner(place, slot):
    y_lo, x, core = place
    dx, dy = slot
    return ((y_lo + dy) % 2) * 4 + (x + 4 + dx * (1 - 2 * core)) % 4


CALLS = (((0, 0), (0, 1)), ((3, 0), (1, 0)), ((3, 1), (1, 1), (2, 0)), ((2, 1),))
SLOTS = tuple((call, k, slot) for call, slots in enumerate(CALLS) for k, slot in enumerate(slots))


def products(scale, s0, s1, targets, scores, row_part):
    count = targets.shape[0]
    rate = scale / math.log(2.0)
    running = None
    for i in range(8):
        source = (s0 if i < 4 else s1)[pl.ds((i % 4) * 256, 256), :]
        part = lax.dot_general(
            targets, source, (((1,), (1,)), ((), ())), preferred_element_type=jnp.float32
        )
        scores[:, pl.ds(i * 256, 256)] = part
        top = jnp.max(part, axis=0, keepdims=True)
        total = jnp.sum(jnp.exp2((part - top) * rate), axis=0, keepdims=True)
        result = top * scale + jnp.log(total)
        row_part[pl.ds(2 * i, 1), :] = result[:, :LANES]
        row_part[pl.ds(2 * i + 1, 1), :] = result[:, LANES:]
        top = jnp.maximum(part[:, :LANES], part[:, LANES:])
        running = top if running is None else jnp.maximum(running, top)
    top = jnp.max(running, axis=1, keepdims=True)
    total = jnp.zeros((count, LANES), jnp.float32)
    for j in range(16):
        total += jnp.exp2((scores[:, pl.ds(j * LANES, LANES)] - top) * rate)
    result = top * scale + jnp.log(jnp.sum(total, axis=1, keepdims=True))
    return [as_row(result[k : k + LANES]) for k in range(0, count, LANES)]


def bring_kernel(sources, targets, sources_here, targets_here, sems):
    copies = [pltpu.make_async_copy(targets, targets_here, sems.at[0])]
    for i in range(8):
        rows = pl.ds(i * 128, 128)
        copies.append(pltpu.make_async_copy(sources.at[rows], sources_here.at[rows], sems.at[i + 1]))
    for copy in copies:
        copy.start()
    for copy in copies:
        copy.wait()


def some_kernel(scale, s0, s1, *refs):
    blocks, (scores, row_part, col_part) = refs[:-3], refs[-3:]
    targets = jnp.concatenate([block[...] for block in blocks], axis=0)
    for k, row in enumerate(products(scale, s0, s1, targets, scores, row_part)):
        col_part[pl.ds(k, 1), :] = row


def end_kernel(scale, s0, s1, ta, *refs):
    rows, cols = refs[:3], refs[3:6]
    scores, joint, sent, scratch, last = refs[6:]
    (col,) = products(scale, s0, s1, ta[...], scores, last)
    joint[...] = log_sum([row[...] for row in rows] + [last[...]])
    place = own_place()
    for call, k, slot in SLOTS:
        row = col if call == 3 else cols[call][pl.ds(k, 1), :]
        scratch[pl.ds(owner(place, slot), 1), :] = row
    whole = scratch[...]
    for e in range(GROUP):
        sent[pl.ds(e * GROUP, GROUP), :] = whole


def log_sum(parts):
    top = functools.reduce(jnp.maximum, parts)
    return top + jnp.log(sum(jnp.exp(part - top) for part in parts))


def row_best_kernel(scale, a0, a1, a2, a3, received, row_joint, own, other, col_norm):
    norm = log_sum([received[pl.ds(e * GROUP, GROUP), :] for e in range(GROUP)])
    col_norm[...] = norm
    place = own_place()
    half = 0.5 / scale
    best = [None] * 16
    for call, k, slot in SLOTS:
        column = as_column(col_norm[pl.ds(owner(place, slot), 1), :]) * half
        column = jnp.broadcast_to(column, (LANES, LANES))
        block = (a0, a1, a2, a3)[call]
        for j in range(16):
            part = block[pl.ds(k * LANES, LANES), pl.ds(j * LANES, LANES)] - column
            part = functools.reduce(jnp.maximum, [part[8 * q : 8 * q + 8] for q in range(16)])
            best[j] = part if best[j] is None else jnp.maximum(best[j], part)
    for j in range(16):
        out = own if j < 8 else other
        out[pl.ds(8 + j % 8, 1), :] = jnp.max(best[j], axis=0, keepdims=True) * scale
    own[:8] = row_joint[:8]
    other[:8] = row_joint[8:]


def join_kernel(own, incoming, sent):
    norm = log_sum([own[:8], incoming[:8]])
    best = jnp.maximum(own[8:], incoming[8:])
    for e in range(16):
        sent[pl.ds(e * 16, 8), :] = norm
        sent[pl.ds(e * 16 + 8, 8), :] = best


def row_norm_kernel(received, row_norm, row_best):
    norm = log_sum([received[pl.ds(e * 16, 8), :] for e in range(16)])
    best = functools.reduce(jnp.maximum, [received[pl.ds(e * 16 + 8, 8), :] for e in range(16)])
    row_norm[...] = norm
    row_best[...] = best - 0.5 * norm


def col_best_kernel(scale, a0, a1, a2, a3, norm_own, norm_other, sent):
    place = own_place()
    half = 0.5 / scale
    own, other = norm_own[...] * half, norm_other[...] * half
    for call, k, slot in SLOTS:
        block = (a0, a1, a2, a3)[call]
        best = None
        for j in range(16):
            norm = (own if j < 8 else other)[j % 8 : j % 8 + 1, :]
            part = block[pl.ds(k * LANES, LANES), pl.ds(j * LANES, LANES)] - norm
            best = part if best is None else jnp.maximum(best, part)
        best = as_row(jnp.max(best, axis=1, keepdims=True)) * scale
        sent[pl.ds(owner(place, slot), 1), :] = best


def last_kernel(received, col_norm, col_best):
    y_lo, x, _ = own_place()
    best = jnp.max(received[...], axis=0, keepdims=True)
    col_best[...] = best - 0.5 * col_norm[pl.ds(y_lo * 4 + x, 1), :]


def body(sources, targets):
    scale = 1.0 / math.sqrt(sources.shape[1])
    groups = column_groups()

    def exchange(value):
        return lax.all_to_all(value, BOTH, 0, 0, axis_index_groups=groups, tiled=True)

    def kept(rows):
        return pltpu.VMEM((rows, 2048), jnp.float32)

    blocks = {}
    blocks[3, 0] = move(targets, ahead)
    blocks[0, 1] = move(targets, across)
    other = held(move(sources, to_core))
    sources, blocks[0, 0] = call(
        bring_kernel,
        (pltpu.VMEM((1024, 1024), jnp.bfloat16), pltpu.VMEM((LANES, 1024), jnp.bfloat16)),
        pltpu.with_memory_space_constraint(sources, pltpu.HBM),
        pltpu.with_memory_space_constraint(targets, pltpu.HBM),
        far=(0, 1),
        scratch=[pltpu.SemaphoreType.DMA((9,))],
    )
    blocks[1, 0] = move(blocks[0, 0], behind)
    blocks[2, 0] = move(blocks[3, 0], ahead)
    blocks[3, 1] = move(blocks[3, 0], across)
    both = (held(sources), other)

    scores, rows, cols = [], [], []
    for n, slots in enumerate(CALLS[:-1]):
        count = len(slots) * LANES
        if n == 1:
            blocks[1, 0], rows[0] = after((blocks[1, 0], rows[0]))
            blocks[1, 1] = move(blocks[1, 0], across)
        if n == 2:
            blocks[2, 0], rows[1] = after((blocks[2, 0], rows[1]))
            blocks[2, 1] = move(blocks[2, 0], across)
        part, row, col = call(
            functools.partial(some_kernel, scale),
            (kept(count), f32(16, LANES), f32(len(slots), LANES)),
            *both,
            *[blocks[slot] for slot in slots],
            flops=2 * count * 2048 * 1024,
            exps=2 * count * 2048,
        )
        scores.append(held(part))
        rows.append(row)
        cols.append(col)
    part, row_joint, sent = call(
        functools.partial(end_kernel, scale),
        (kept(LANES), f32(16, LANES), f32(GROUP * GROUP, LANES)),
        *both,
        blocks[CALLS[-1][0]],
        *rows,
        *cols,
        flops=2 * LANES * 2048 * 1024,
        exps=2 * LANES * 2048,
        scratch=[pltpu.VMEM((GROUP, LANES), jnp.float32), pltpu.VMEM((16, LANES), jnp.float32)],
    )
    scores.append(held(part))
    received = exchange(sent)
    own, other, col_norm = call(
        functools.partial(row_best_kernel, scale),
        (f32(16, LANES), f32(16, LANES), f32(GROUP, LANES)),
        *scores,
        received,
        row_joint,
        flops=2 * 1024 * 2048,
    )
    sent = call(join_kernel, f32(256, LANES), own, move(other, to_core))
    received = lax.all_to_all(sent, "wide", 0, 0, tiled=True)
    row_norm, row_best = call(row_norm_kernel, (f32(8, LANES), f32(8, LANES)), received)
    sent = call(
        functools.partial(col_best_kernel, scale),
        f32(GROUP, LANES),
        *scores,
        row_norm,
        move(row_norm, to_core),
        flops=2 * 1024 * 2048,
    )
    received = exchange(sent)
    col_best = call(last_kernel, f32(1, LANES), received, col_norm)
    return row_best.reshape(1024), col_best.reshape(LANES)


def solution(mesh):
    return jax.shard_map(
        body,
        mesh=mesh,
        in_specs=(P("narrow", None), P(("wide", "narrow"), None)),
        out_specs=(P("narrow"), P(("wide", "narrow"))),
        check_vma=False,
    )
```

```python
import functools
import math

import jax
import jax.numpy as jnp
from jax import lax
from jax.experimental import pallas as pl
from jax.experimental.pallas import tpu as pltpu
from jax.sharding import PartitionSpec as P

XS, YS, ZS, CORES = 4, 4, 8, 2
BOTH = ("wide", "narrow")
GROUP = 8
LANES = 128


def device_index(z, y, x, core):
    y, x, z = y % YS, x % XS, z % ZS
    return (z * 2 + y // 2) * 16 + (y % 2) * 8 + x * 2 + core


def places():
    for z in range(ZS):
        for y in range(YS):
            for x in range(XS):
                for core in range(CORES):
                    yield z, y, x, core


def partner(y, core):
    return y ^ 1 if core == 0 else 3 - y


def move(value, where):
    pairs = [(device_index(*place), device_index(*where(*place))) for place in places()]
    return lax.ppermute(value, BOTH, pairs)


def ahead(z, y, x, core):
    return z, y, x + 1 - 2 * core, core


def behind(z, y, x, core):
    return z, y, x - 1 + 2 * core, core


def across(z, y, x, core):
    return z, partner(y, core), x, core


def to_core(z, y, x, core):
    return z, y, x, 1 - core


def column_groups():
    groups = []
    for z in range(ZS):
        for core in range(CORES):
            for y in (0, 2):
                rows = (y, partner(y, core))
                groups.append([device_index(z, row, x, core) for row in rows for x in range(XS)])
    return groups


def vmem():
    return pl.BlockSpec(memory_space=pltpu.VMEM)


def after(values):
    return lax.optimization_barrier(values)


def held(value):
    return pltpu.with_memory_space_constraint(value, pltpu.VMEM)


def call(kernel, out_shape, *operands, flops=0, exps=0, scratch=(), far=(), limit=24):
    moved = sum(math.prod(o.shape) * o.dtype.itemsize for o in operands)
    return pl.pallas_call(
        kernel,
        out_shape=out_shape,
        in_specs=[pl.BlockSpec(memory_space=pltpu.HBM) if k in far else vmem() for k in range(len(operands))],
        out_specs=jax.tree.map(lambda _: vmem(), out_shape),
        scratch_shapes=list(scratch),
        cost_estimate=pl.CostEstimate(flops=flops, bytes_accessed=moved, transcendentals=exps),
        compiler_params=pltpu.CompilerParams(vmem_limit_bytes=limit * 1024 * 1024),
    )(*operands)


def f32(*shape):
    return jax.ShapeDtypeStruct(shape, jnp.float32)


def eye():
    row = lax.broadcasted_iota(jnp.int32, (LANES, LANES), 0)
    return row == lax.broadcasted_iota(jnp.int32, (LANES, LANES), 1)


def as_row(column):
    return jnp.sum(jnp.where(eye(), column, 0.0), axis=0, keepdims=True)


def as_column(row):
    return jnp.sum(jnp.where(eye(), row, 0.0), axis=1, keepdims=True)


def own_place():
    narrow = lax.axis_index("narrow")
    return narrow // 8, (narrow // 2) % 4, narrow % 2


def owner(place, slot):
    y_lo, x, core = place
    dx, dy = slot
    return ((y_lo + dy) % 2) * 4 + (x + 4 + dx * (1 - 2 * core)) % 4


CALLS = (((0, 0), (0, 1)), ((3, 0), (1, 0)), ((3, 1), (2, 0)), ((1, 1), (2, 1)))
SLOTS = tuple((call, k, slot) for call, slots in enumerate(CALLS) for k, slot in enumerate(slots))


def products(scale, s0, s1, targets, scores, row_part):
    count = targets.shape[0]
    rate = scale / math.log(2.0)
    running = None
    for i in range(8):
        source = (s0 if i < 4 else s1)[pl.ds((i % 4) * 256, 256), :]
        part = lax.dot_general(
            targets, source, (((1,), (1,)), ((), ())), preferred_element_type=jnp.float32
        )
        scores[:, pl.ds(i * 256, 256)] = part
        top = jnp.max(part, axis=0, keepdims=True)
        total = jnp.sum(jnp.exp2((part - top) * rate), axis=0, keepdims=True)
        result = top * scale + jnp.log(total)
        row_part[pl.ds(2 * i, 1), :] = result[:, :LANES]
        row_part[pl.ds(2 * i + 1, 1), :] = result[:, LANES:]
        top = jnp.maximum(part[:, :LANES], part[:, LANES:])
        running = top if running is None else jnp.maximum(running, top)
    top = jnp.max(running, axis=1, keepdims=True)
    total = jnp.zeros((count, LANES), jnp.float32)
    for j in range(16):
        total += jnp.exp2((scores[:, pl.ds(j * LANES, LANES)] - top) * rate)
    result = top * scale + jnp.log(jnp.sum(total, axis=1, keepdims=True))
    return [as_row(result[k : k + LANES]) for k in range(0, count, LANES)]


def bring_kernel(sources, targets, sources_here, targets_here, sems):
    copies = [pltpu.make_async_copy(targets, targets_here, sems.at[0])]
    for i in range(8):
        rows = pl.ds(i * 128, 128)
        copies.append(pltpu.make_async_copy(sources.at[rows], sources_here.at[rows], sems.at[i + 1]))
    for copy in copies:
        copy.start()
    for copy in copies:
        copy.wait()


def some_kernel(scale, s0, s1, *refs):
    blocks, (scores, row_part, col_part) = refs[:-3], refs[-3:]
    targets = jnp.concatenate([block[...] for block in blocks], axis=0)
    for k, row in enumerate(products(scale, s0, s1, targets, scores, row_part)):
        col_part[pl.ds(k, 1), :] = row


def end_kernel(scale, s0, s1, ta, tb, *refs):
    rows, cols = refs[:3], refs[3:6]
    scores, joint, sent, scratch, last = refs[6:]
    targets = jnp.concatenate([ta[...], tb[...]], axis=0)
    ends = products(scale, s0, s1, targets, scores, last)
    joint[...] = log_sum([row[...] for row in rows] + [last[...]])
    place = own_place()
    for call, k, slot in SLOTS:
        row = ends[k] if call == 3 else cols[call][pl.ds(k, 1), :]
        scratch[pl.ds(owner(place, slot), 1), :] = row
    whole = scratch[...]
    for e in range(GROUP):
        sent[pl.ds(e * GROUP, GROUP), :] = whole


def log_sum(parts):
    top = functools.reduce(jnp.maximum, parts)
    return top + jnp.log(sum(jnp.exp(part - top) for part in parts))


def row_best_kernel(scale, a0, a1, a2, a3, received, row_joint, rows, col_norm):
    norm = log_sum([received[pl.ds(e * GROUP, GROUP), :] for e in range(GROUP)])
    col_norm[...] = norm
    place = own_place()
    half = 0.5 / scale
    best = [None] * 16
    for call, k, slot in SLOTS:
        column = as_column(col_norm[pl.ds(owner(place, slot), 1), :]) * half
        column = jnp.broadcast_to(column, (LANES, LANES))
        block = (a0, a1, a2, a3)[call]
        for j in range(16):
            part = block[pl.ds(k * LANES, LANES), pl.ds(j * LANES, LANES)] - column
            part = functools.reduce(jnp.maximum, [part[8 * q : 8 * q + 8] for q in range(16)])
            best[j] = part if best[j] is None else jnp.maximum(best[j], part)
    rows[:16] = row_joint[...]
    for j in range(16):
        rows[pl.ds(16 + j, 1), :] = jnp.max(best[j], axis=0, keepdims=True) * scale


def join_kernel(rows, incoming, sent):
    norm_own = log_sum([rows[:8], incoming[8:16]])
    norm_other = log_sum([rows[8:16], incoming[:8]])
    best_own = jnp.maximum(rows[16:24], incoming[24:])
    best_other = jnp.maximum(rows[24:], incoming[16:24])
    for e in range(16):
        for k, value in enumerate((norm_own, norm_other, best_own, best_other)):
            sent[pl.ds(e * 32 + k * 8, 8), :] = value


def col_best_kernel(scale, a0, a1, a2, a3, received, col_norm, sent, row_best):
    parts = [received[pl.ds(e * 32, 16), :] for e in range(16)]
    row_norm = log_sum(parts)
    best = functools.reduce(jnp.maximum, [received[pl.ds(e * 32 + 16, 8), :] for e in range(16)])
    row_best[...] = best - 0.5 * row_norm[:8]
    place = own_place()
    norms = row_norm * (0.5 / scale)
    for call, k, slot in SLOTS:
        block = (a0, a1, a2, a3)[call]
        best = None
        for j in range(16):
            part = block[pl.ds(k * LANES, LANES), pl.ds(j * LANES, LANES)] - norms[j : j + 1, :]
            best = part if best is None else jnp.maximum(best, part)
        best = as_row(jnp.max(best, axis=1, keepdims=True)) * scale
        position = owner(place, slot)
        sent[pl.ds(position, 1), :] = best - 0.5 * col_norm[pl.ds(position, 1), :]


def last_kernel(received, row_best_held, row_best, col_best):
    row_best[...] = row_best_held[...]
    col_best[...] = jnp.max(received[...], axis=0, keepdims=True)


def body(sources, targets):
    scale = 1.0 / math.sqrt(sources.shape[1])
    groups = column_groups()

    def exchange(value):
        return lax.all_to_all(value, BOTH, 0, 0, axis_index_groups=groups, tiled=True)

    def kept(rows):
        return pltpu.VMEM((rows, 2048), jnp.float32)

    blocks = {}
    blocks[3, 0] = move(targets, ahead)
    blocks[0, 1] = move(targets, across)
    other = held(move(sources, to_core))
    sources, blocks[0, 0] = call(
        bring_kernel,
        (pltpu.VMEM((1024, 1024), jnp.bfloat16), pltpu.VMEM((LANES, 1024), jnp.bfloat16)),
        pltpu.with_memory_space_constraint(sources, pltpu.HBM),
        pltpu.with_memory_space_constraint(targets, pltpu.HBM),
        far=(0, 1),
        scratch=[pltpu.SemaphoreType.DMA((9,))],
    )
    blocks[1, 0] = move(blocks[0, 0], behind)
    blocks[3, 0], blocks[0, 0] = after((blocks[3, 0], blocks[0, 0]))
    blocks[2, 0] = move(blocks[3, 0], ahead)
    blocks[3, 1] = move(blocks[3, 0], across)
    both = (held(sources), other)

    scores, rows, cols = [], [], []
    for n, slots in enumerate(CALLS[:-1]):
        count = len(slots) * LANES
        if n == 1:
            blocks[1, 0], rows[0] = after((blocks[1, 0], rows[0]))
            blocks[1, 1] = move(blocks[1, 0], across)
        if n == 2:
            blocks[2, 0], rows[1] = after((blocks[2, 0], rows[1]))
            blocks[2, 1] = move(blocks[2, 0], across)
        part, row, col = call(
            functools.partial(some_kernel, scale),
            (kept(count), f32(16, LANES), f32(len(slots), LANES)),
            *both,
            *[blocks[slot] for slot in slots],
            flops=2 * count * 2048 * 1024,
            exps=2 * count * 2048,
        )
        scores.append(held(part))
        rows.append(row)
        cols.append(col)
    part, row_joint, sent = call(
        functools.partial(end_kernel, scale),
        (kept(2 * LANES), f32(16, LANES), f32(GROUP * GROUP, LANES)),
        *both,
        *[blocks[slot] for slot in CALLS[-1]],
        *rows,
        *cols,
        flops=4 * LANES * 2048 * 1024,
        exps=4 * LANES * 2048,
        scratch=[pltpu.VMEM((GROUP, LANES), jnp.float32), pltpu.VMEM((16, LANES), jnp.float32)],
    )
    scores.append(held(part))
    received = exchange(sent)
    joint, col_norm = call(
        functools.partial(row_best_kernel, scale),
        (f32(32, LANES), f32(GROUP, LANES)),
        *scores,
        received,
        row_joint,
        flops=2 * 1024 * 2048,
    )
    sent = call(join_kernel, f32(512, LANES), joint, move(joint, to_core))
    received = lax.all_to_all(sent, "wide", 0, 0, tiled=True)
    sent, row_best = call(
        functools.partial(col_best_kernel, scale),
        (f32(GROUP, LANES), pltpu.VMEM((8, LANES), jnp.float32)),
        *scores,
        received,
        col_norm,
        flops=2 * 1024 * 2048,
    )
    received = exchange(sent)
    row_best, col_best = call(
        last_kernel, (f32(8, LANES), f32(1, LANES)), received, held(row_best)
    )
    return row_best.reshape(1024), col_best.reshape(LANES)


def solution(mesh):
    return jax.shard_map(
        body,
        mesh=mesh,
        in_specs=(P("narrow", None), P(("wide", "narrow"), None)),
        out_specs=(P("narrow"), P(("wide", "narrow"))),
        check_vma=False,
    )
```

```python
import functools
import math

import jax
import jax.numpy as jnp
from jax import lax
from jax.experimental import pallas as pl
from jax.experimental.pallas import tpu as pltpu
from jax.sharding import PartitionSpec as P

XS, YS, ZS, CORES = 4, 4, 8, 2
BOTH = ("wide", "narrow")
GROUP = 8
LANES = 128


def device_index(z, y, x, core):
    y, x, z = y % YS, x % XS, z % ZS
    return (z * 2 + y // 2) * 16 + (y % 2) * 8 + x * 2 + core


def places():
    for z in range(ZS):
        for y in range(YS):
            for x in range(XS):
                for core in range(CORES):
                    yield z, y, x, core


def partner(y, core):
    return y ^ 1 if core == 0 else 3 - y


def move(value, where):
    pairs = [(device_index(*place), device_index(*where(*place))) for place in places()]
    return lax.ppermute(value, BOTH, pairs)


def ahead(z, y, x, core):
    return z, y, x + 1 - 2 * core, core


def behind(z, y, x, core):
    return z, y, x - 1 + 2 * core, core


def across(z, y, x, core):
    return z, partner(y, core), x, core


def ahead_across(z, y, x, core):
    return z, partner(y, core), x + 1 - 2 * core, core


def to_core(z, y, x, core):
    return z, y, x, 1 - core


def column_groups():
    groups = []
    for z in range(ZS):
        for core in range(CORES):
            for y in (0, 2):
                rows = (y, partner(y, core))
                groups.append([device_index(z, row, x, core) for row in rows for x in range(XS)])
    return groups


def vmem():
    return pl.BlockSpec(memory_space=pltpu.VMEM)


def after(values):
    return lax.optimization_barrier(values)


def held(value):
    return pltpu.with_memory_space_constraint(value, pltpu.VMEM)


def call(kernel, out_shape, *operands, flops=0, exps=0, scratch=(), far=(), limit=24):
    moved = sum(math.prod(o.shape) * o.dtype.itemsize for o in operands)
    return pl.pallas_call(
        kernel,
        out_shape=out_shape,
        in_specs=[pl.BlockSpec(memory_space=pltpu.HBM) if k in far else vmem() for k in range(len(operands))],
        out_specs=jax.tree.map(lambda _: vmem(), out_shape),
        scratch_shapes=list(scratch),
        cost_estimate=pl.CostEstimate(flops=flops, bytes_accessed=moved, transcendentals=exps),
        compiler_params=pltpu.CompilerParams(vmem_limit_bytes=limit * 1024 * 1024),
    )(*operands)


def f32(*shape):
    return jax.ShapeDtypeStruct(shape, jnp.float32)


def eye():
    row = lax.broadcasted_iota(jnp.int32, (LANES, LANES), 0)
    return row == lax.broadcasted_iota(jnp.int32, (LANES, LANES), 1)


def as_row(column):
    return jnp.sum(jnp.where(eye(), column, 0.0), axis=0, keepdims=True)


def as_column(row):
    return jnp.sum(jnp.where(eye(), row, 0.0), axis=1, keepdims=True)


def own_place():
    narrow = lax.axis_index("narrow")
    return narrow // 8, (narrow // 2) % 4, narrow % 2


def owner(place, slot):
    y_lo, x, core = place
    dx, dy = slot
    return ((y_lo + dy) % 2) * 4 + (x + 4 + dx * (1 - 2 * core)) % 4


CALLS = (((0, 0), (0, 1)), ((3, 0), (1, 0)), ((3, 1), (2, 0)), ((1, 1), (2, 1)))
SLOTS = tuple((call, k, slot) for call, slots in enumerate(CALLS) for k, slot in enumerate(slots))


def products(scale, s0, s1, targets, scores, row_part):
    count = targets.shape[0]
    rate = scale / math.log(2.0)
    running = None
    for i in range(8):
        source = (s0 if i < 4 else s1)[pl.ds((i % 4) * 256, 256), :]
        part = lax.dot_general(
            targets, source, (((1,), (1,)), ((), ())), preferred_element_type=jnp.float32
        )
        scores[:, pl.ds(i * 256, 256)] = part
        top = jnp.max(part, axis=0, keepdims=True)
        total = jnp.sum(jnp.exp2((part - top) * rate), axis=0, keepdims=True)
        result = top * scale + jnp.log(total)
        row_part[pl.ds(2 * i, 1), :] = result[:, :LANES]
        row_part[pl.ds(2 * i + 1, 1), :] = result[:, LANES:]
        top = jnp.maximum(part[:, :LANES], part[:, LANES:])
        running = top if running is None else jnp.maximum(running, top)
    top = jnp.max(running, axis=1, keepdims=True)
    total = jnp.zeros((count, LANES), jnp.float32)
    for j in range(16):
        total += jnp.exp2((scores[:, pl.ds(j * LANES, LANES)] - top) * rate)
    result = top * scale + jnp.log(jnp.sum(total, axis=1, keepdims=True))
    return [as_row(result[k : k + LANES]) for k in range(0, count, LANES)]


def bring_kernel(sources, targets, sources_here, targets_here, sems):
    copies = [pltpu.make_async_copy(targets, targets_here, sems.at[0])]
    for i in range(8):
        rows = pl.ds(i * 128, 128)
        copies.append(pltpu.make_async_copy(sources.at[rows], sources_here.at[rows], sems.at[i + 1]))
    for copy in copies:
        copy.start()
    for copy in copies:
        copy.wait()


def some_kernel(scale, s0, s1, *refs):
    blocks, (scores, row_part, col_part) = refs[:-3], refs[-3:]
    targets = jnp.concatenate([block[...] for block in blocks], axis=0)
    for k, row in enumerate(products(scale, s0, s1, targets, scores, row_part)):
        col_part[pl.ds(k, 1), :] = row


def end_kernel(scale, s0, s1, ta, tb, *refs):
    rows, cols = refs[:3], refs[3:6]
    scores, joint, sent, scratch, last = refs[6:]
    targets = jnp.concatenate([ta[...], tb[...]], axis=0)
    ends = products(scale, s0, s1, targets, scores, last)
    joint[...] = log_sum([row[...] for row in rows] + [last[...]])
    place = own_place()
    for call, k, slot in SLOTS:
        row = ends[k] if call == 3 else cols[call][pl.ds(k, 1), :]
        scratch[pl.ds(owner(place, slot), 1), :] = row
    whole = scratch[...]
    for e in range(GROUP):
        sent[pl.ds(e * GROUP, GROUP), :] = whole


def log_sum(parts):
    top = functools.reduce(jnp.maximum, parts)
    return top + jnp.log(sum(jnp.exp(part - top) for part in parts))


def row_best_kernel(scale, a0, a1, a2, a3, received, row_joint, rows, col_norm):
    norm = log_sum([received[pl.ds(e * GROUP, GROUP), :] for e in range(GROUP)])
    col_norm[...] = norm
    place = own_place()
    half = 0.5 / scale
    best = [None] * 16
    for call, k, slot in SLOTS:
        column = as_column(col_norm[pl.ds(owner(place, slot), 1), :]) * half
        column = jnp.broadcast_to(column, (LANES, LANES))
        block = (a0, a1, a2, a3)[call]
        for j in range(16):
            part = block[pl.ds(k * LANES, LANES), pl.ds(j * LANES, LANES)] - column
            part = functools.reduce(jnp.maximum, [part[8 * q : 8 * q + 8] for q in range(16)])
            best[j] = part if best[j] is None else jnp.maximum(best[j], part)
    rows[:16] = row_joint[...]
    for j in range(16):
        rows[pl.ds(16 + j, 1), :] = jnp.max(best[j], axis=0, keepdims=True) * scale


def join_kernel(rows, incoming, sent):
    norm_own = log_sum([rows[:8], incoming[8:16]])
    norm_other = log_sum([rows[8:16], incoming[:8]])
    best_own = jnp.maximum(rows[16:24], incoming[24:])
    best_other = jnp.maximum(rows[24:], incoming[16:24])
    for e in range(16):
        for k, value in enumerate((norm_own, norm_other, best_own, best_other)):
            sent[pl.ds(e * 32 + k * 8, 8), :] = value


def col_best_kernel(scale, a0, a1, a2, a3, received, col_norm, sent, row_best):
    parts = [received[pl.ds(e * 32, 16), :] for e in range(16)]
    row_norm = log_sum(parts)
    best = functools.reduce(jnp.maximum, [received[pl.ds(e * 32 + 16, 8), :] for e in range(16)])
    row_best[...] = best - 0.5 * row_norm[:8]
    place = own_place()
    norms = row_norm * (0.5 / scale)
    for call, k, slot in SLOTS:
        block = (a0, a1, a2, a3)[call]
        best = None
        for j in range(16):
            part = block[pl.ds(k * LANES, LANES), pl.ds(j * LANES, LANES)] - norms[j : j + 1, :]
            best = part if best is None else jnp.maximum(best, part)
        best = as_row(jnp.max(best, axis=1, keepdims=True)) * scale
        position = owner(place, slot)
        sent[pl.ds(position, 1), :] = best - 0.5 * col_norm[pl.ds(position, 1), :]


def last_kernel(received, row_best_held, row_best, col_best):
    row_best[...] = row_best_held[...]
    col_best[...] = jnp.max(received[...], axis=0, keepdims=True)


def body(sources, targets):
    scale = 1.0 / math.sqrt(sources.shape[1])
    groups = column_groups()

    def exchange(value):
        return lax.all_to_all(value, BOTH, 0, 0, axis_index_groups=groups, tiled=True)

    def kept(rows):
        return pltpu.VMEM((rows, 2048), jnp.float32)

    blocks = {}
    blocks[3, 0] = move(targets, ahead)
    blocks[0, 1] = move(targets, across)
    other = held(move(sources, to_core))
    sources, blocks[0, 0] = call(
        bring_kernel,
        (pltpu.VMEM((1024, 1024), jnp.bfloat16), pltpu.VMEM((LANES, 1024), jnp.bfloat16)),
        pltpu.with_memory_space_constraint(sources, pltpu.HBM),
        pltpu.with_memory_space_constraint(targets, pltpu.HBM),
        far=(0, 1),
        scratch=[pltpu.SemaphoreType.DMA((9,))],
    )
    blocks[1, 0] = move(blocks[0, 0], behind)
    blocks[3, 0], blocks[0, 0] = after((blocks[3, 0], blocks[0, 0]))
    blocks[2, 1] = move(blocks[3, 0], ahead_across)
    blocks[2, 0] = move(blocks[3, 0], ahead)
    blocks[3, 1] = move(blocks[3, 0], across)
    both = (held(sources), other)

    scores, rows, cols = [], [], []
    for n, slots in enumerate(CALLS[:-1]):
        count = len(slots) * LANES
        if n == 1:
            blocks[1, 0], rows[0] = after((blocks[1, 0], rows[0]))
            blocks[1, 1] = move(blocks[1, 0], across)
        part, row, col = call(
            functools.partial(some_kernel, scale),
            (kept(count), f32(16, LANES), f32(len(slots), LANES)),
            *both,
            *[blocks[slot] for slot in slots],
            flops=2 * count * 2048 * 1024,
            exps=2 * count * 2048,
        )
        scores.append(held(part))
        rows.append(row)
        cols.append(col)
    part, row_joint, sent = call(
        functools.partial(end_kernel, scale),
        (kept(2 * LANES), f32(16, LANES), f32(GROUP * GROUP, LANES)),
        *both,
        *[blocks[slot] for slot in CALLS[-1]],
        *rows,
        *cols,
        flops=4 * LANES * 2048 * 1024,
        exps=4 * LANES * 2048,
        scratch=[pltpu.VMEM((GROUP, LANES), jnp.float32), pltpu.VMEM((16, LANES), jnp.float32)],
    )
    scores.append(held(part))
    received = exchange(sent)
    joint, col_norm = call(
        functools.partial(row_best_kernel, scale),
        (f32(32, LANES), f32(GROUP, LANES)),
        *scores,
        received,
        row_joint,
        flops=2 * 1024 * 2048,
    )
    sent = call(join_kernel, f32(512, LANES), joint, move(joint, to_core))
    received = lax.all_to_all(sent, "wide", 0, 0, tiled=True)
    sent, row_best = call(
        functools.partial(col_best_kernel, scale),
        (f32(GROUP, LANES), pltpu.VMEM((8, LANES), jnp.float32)),
        *scores,
        received,
        col_norm,
        flops=2 * 1024 * 2048,
    )
    received = exchange(sent)
    row_best, col_best = call(
        last_kernel, (f32(8, LANES), f32(1, LANES)), received, held(row_best)
    )
    return row_best.reshape(1024), col_best.reshape(LANES)


def solution(mesh):
    return jax.shard_map(
        body,
        mesh=mesh,
        in_specs=(P("narrow", None), P(("wide", "narrow"), None)),
        out_specs=(P("narrow"), P(("wide", "narrow"))),
        check_vma=False,
    )
```

```python
import functools
import math

import jax
import jax.numpy as jnp
from jax import lax
from jax.experimental import pallas as pl
from jax.experimental.pallas import tpu as pltpu
from jax.sharding import PartitionSpec as P

XS, YS, ZS, CORES = 4, 4, 8, 2
BOTH = ("wide", "narrow")
GROUP = 8
LANES = 128


def device_index(z, y, x, core):
    y, x, z = y % YS, x % XS, z % ZS
    return (z * 2 + y // 2) * 16 + (y % 2) * 8 + x * 2 + core


def places():
    for z in range(ZS):
        for y in range(YS):
            for x in range(XS):
                for core in range(CORES):
                    yield z, y, x, core


def partner(y, core):
    return y ^ 1 if core == 0 else 3 - y


def move(value, where):
    pairs = [(device_index(*place), device_index(*where(*place))) for place in places()]
    return lax.ppermute(value, BOTH, pairs)


def ahead(z, y, x, core):
    return z, y, x + 1 - 2 * core, core


def behind(z, y, x, core):
    return z, y, x - 1 + 2 * core, core


def across(z, y, x, core):
    return z, partner(y, core), x, core


def ahead_across(z, y, x, core):
    return z, partner(y, core), x + 1 - 2 * core, core


def to_core(z, y, x, core):
    return z, y, x, 1 - core


def to_far(z, y, x, core):
    return z, y + 2, x, core


def column_groups():
    groups = []
    for z in range(ZS):
        for core in range(CORES):
            for y in (0, 2):
                rows = (y, partner(y, core))
                groups.append([device_index(z, row, x, core) for row in rows for x in range(XS)])
    return groups


def vmem():
    return pl.BlockSpec(memory_space=pltpu.VMEM)


def after(values):
    return lax.optimization_barrier(values)


def held(value):
    return pltpu.with_memory_space_constraint(value, pltpu.VMEM)


def call(kernel, out_shape, *operands, flops=0, exps=0, scratch=(), far=(), limit=24):
    moved = sum(math.prod(o.shape) * o.dtype.itemsize for o in operands)
    return pl.pallas_call(
        kernel,
        out_shape=out_shape,
        in_specs=[pl.BlockSpec(memory_space=pltpu.HBM) if k in far else vmem() for k in range(len(operands))],
        out_specs=jax.tree.map(lambda _: vmem(), out_shape),
        scratch_shapes=list(scratch),
        cost_estimate=pl.CostEstimate(flops=flops, bytes_accessed=moved, transcendentals=exps),
        compiler_params=pltpu.CompilerParams(vmem_limit_bytes=limit * 1024 * 1024),
    )(*operands)


def f32(*shape):
    return jax.ShapeDtypeStruct(shape, jnp.float32)


def eye():
    row = lax.broadcasted_iota(jnp.int32, (LANES, LANES), 0)
    return row == lax.broadcasted_iota(jnp.int32, (LANES, LANES), 1)


def as_row(column):
    return jnp.sum(jnp.where(eye(), column, 0.0), axis=0, keepdims=True)


def as_column(row):
    return jnp.sum(jnp.where(eye(), row, 0.0), axis=1, keepdims=True)


def own_place():
    narrow = lax.axis_index("narrow")
    return narrow // 8, (narrow // 2) % 4, narrow % 2


def owner(place, slot):
    y_lo, x, core = place
    dx, dy = slot
    return ((y_lo + dy) % 2) * 4 + (x + 4 + dx * (1 - 2 * core)) % 4


CALLS = (((0, 0), (0, 1)), ((3, 0), (1, 0)), ((3, 1), (2, 0)), ((1, 1), (2, 1)))
SLOTS = tuple((call, k, slot) for call, slots in enumerate(CALLS) for k, slot in enumerate(slots))


def products(scale, s0, s1, targets, scores, row_part):
    count = targets.shape[0]
    rate = scale / math.log(2.0)
    running = None
    for i in range(8):
        source = (s0 if i < 4 else s1)[pl.ds((i % 4) * 256, 256), :]
        part = lax.dot_general(
            targets, source, (((1,), (1,)), ((), ())), preferred_element_type=jnp.float32
        )
        scores[:, pl.ds(i * 256, 256)] = part
        top = jnp.max(part, axis=0, keepdims=True)
        total = jnp.sum(jnp.exp2((part - top) * rate), axis=0, keepdims=True)
        result = top * scale + jnp.log(total)
        row_part[pl.ds(2 * i, 1), :] = result[:, :LANES]
        row_part[pl.ds(2 * i + 1, 1), :] = result[:, LANES:]
        top = jnp.maximum(part[:, :LANES], part[:, LANES:])
        running = top if running is None else jnp.maximum(running, top)
    top = jnp.max(running, axis=1, keepdims=True)
    total = jnp.zeros((count, LANES), jnp.float32)
    for j in range(16):
        total += jnp.exp2((scores[:, pl.ds(j * LANES, LANES)] - top) * rate)
    result = top * scale + jnp.log(jnp.sum(total, axis=1, keepdims=True))
    return [as_row(result[k : k + LANES]) for k in range(0, count, LANES)]


def bring_kernel(sources, targets, sources_here, targets_here, sems):
    copies = [pltpu.make_async_copy(targets, targets_here, sems.at[0])]
    for i in range(8):
        rows = pl.ds(i * 128, 128)
        copies.append(pltpu.make_async_copy(sources.at[rows], sources_here.at[rows], sems.at[i + 1]))
    for copy in copies:
        copy.start()
    for copy in copies:
        copy.wait()


def some_kernel(scale, s0, s1, *refs):
    blocks, (scores, row_part, col_part) = refs[:-3], refs[-3:]
    targets = jnp.concatenate([block[...] for block in blocks], axis=0)
    for k, row in enumerate(products(scale, s0, s1, targets, scores, row_part)):
        col_part[pl.ds(k, 1), :] = row


def end_kernel(scale, s0, s1, ta, tb, *refs):
    rows, cols = refs[:3], refs[3:6]
    scores, joint, sent, scratch, last = refs[6:]
    targets = jnp.concatenate([ta[...], tb[...]], axis=0)
    ends = products(scale, s0, s1, targets, scores, last)
    joint[...] = log_sum([row[...] for row in rows] + [last[...]])
    place = own_place()
    for call, k, slot in SLOTS:
        row = ends[k] if call == 3 else cols[call][pl.ds(k, 1), :]
        scratch[pl.ds(owner(place, slot), 1), :] = row
    whole = scratch[...]
    for e in range(GROUP):
        sent[pl.ds(e * GROUP, GROUP), :] = whole


def log_sum(parts):
    top = functools.reduce(jnp.maximum, parts)
    return top + jnp.log(sum(jnp.exp(part - top) for part in parts))


def row_best_kernel(scale, a0, a1, a2, a3, received, row_joint, rows, col_norm):
    norm = log_sum([received[pl.ds(e * GROUP, GROUP), :] for e in range(GROUP)])
    col_norm[...] = norm
    place = own_place()
    half = 0.5 / scale
    best = [None] * 16
    for call, k, slot in SLOTS:
        column = as_column(col_norm[pl.ds(owner(place, slot), 1), :]) * half
        column = jnp.broadcast_to(column, (LANES, LANES))
        block = (a0, a1, a2, a3)[call]
        for j in range(16):
            part = block[pl.ds(k * LANES, LANES), pl.ds(j * LANES, LANES)] - column
            part = functools.reduce(jnp.maximum, [part[8 * q : 8 * q + 8] for q in range(16)])
            best[j] = part if best[j] is None else jnp.maximum(best[j], part)
    rows[:16] = row_joint[...]
    for j in range(16):
        rows[pl.ds(16 + j, 1), :] = jnp.max(best[j], axis=0, keepdims=True) * scale


def core_kernel(rows, core, joint):
    joint[:8] = log_sum([rows[:8], core[8:16]])
    joint[8:16] = log_sum([rows[8:16], core[:8]])
    joint[16:24] = jnp.maximum(rows[16:24], core[24:])
    joint[24:] = jnp.maximum(rows[24:], core[16:24])


def join_kernel(rows, far, sent):
    norm = log_sum([rows[:16], far[:16]])
    best = jnp.maximum(rows[16:], far[16:])
    for e in range(ZS):
        sent[pl.ds(e * 32, 16), :] = norm
        sent[pl.ds(e * 32 + 16, 16), :] = best


def col_best_kernel(scale, a0, a1, a2, a3, received, col_norm, sent, row_best):
    parts = [received[pl.ds(e * 32, 16), :] for e in range(ZS)]
    row_norm = log_sum(parts)
    best = functools.reduce(jnp.maximum, [received[pl.ds(e * 32 + 16, 8), :] for e in range(ZS)])
    row_best[...] = best - 0.5 * row_norm[:8]
    place = own_place()
    norms = row_norm * (0.5 / scale)
    for call, k, slot in SLOTS:
        block = (a0, a1, a2, a3)[call]
        best = None
        for j in range(16):
            part = block[pl.ds(k * LANES, LANES), pl.ds(j * LANES, LANES)] - norms[j : j + 1, :]
            best = part if best is None else jnp.maximum(best, part)
        best = as_row(jnp.max(best, axis=1, keepdims=True)) * scale
        position = owner(place, slot)
        sent[pl.ds(position, 1), :] = best - 0.5 * col_norm[pl.ds(position, 1), :]


def last_kernel(received, row_best_held, row_best, col_best):
    row_best[...] = row_best_held[...]
    col_best[...] = jnp.max(received[...], axis=0, keepdims=True)


def body(sources, targets):
    scale = 1.0 / math.sqrt(sources.shape[1])
    groups = column_groups()

    def exchange(value):
        return lax.all_to_all(value, BOTH, 0, 0, axis_index_groups=groups, tiled=True)

    def kept(rows):
        return pltpu.VMEM((rows, 2048), jnp.float32)

    blocks = {}
    blocks[3, 0] = move(targets, ahead)
    blocks[0, 1] = move(targets, across)
    other = held(move(sources, to_core))
    sources, blocks[0, 0] = call(
        bring_kernel,
        (pltpu.VMEM((1024, 1024), jnp.bfloat16), pltpu.VMEM((LANES, 1024), jnp.bfloat16)),
        pltpu.with_memory_space_constraint(sources, pltpu.HBM),
        pltpu.with_memory_space_constraint(targets, pltpu.HBM),
        far=(0, 1),
        scratch=[pltpu.SemaphoreType.DMA((9,))],
    )
    blocks[1, 0] = move(blocks[0, 0], behind)
    blocks[3, 0], blocks[0, 0] = after((blocks[3, 0], blocks[0, 0]))
    blocks[2, 1] = move(blocks[3, 0], ahead_across)
    blocks[2, 0] = move(blocks[3, 0], ahead)
    blocks[3, 1] = move(blocks[3, 0], across)
    both = (held(sources), other)

    scores, rows, cols = [], [], []
    for n, slots in enumerate(CALLS[:-1]):
        count = len(slots) * LANES
        if n == 1:
            blocks[1, 0], rows[0] = after((blocks[1, 0], rows[0]))
            blocks[1, 1] = move(blocks[1, 0], across)
        part, row, col = call(
            functools.partial(some_kernel, scale),
            (kept(count), f32(16, LANES), f32(len(slots), LANES)),
            *both,
            *[blocks[slot] for slot in slots],
            flops=2 * count * 2048 * 1024,
            exps=2 * count * 2048,
        )
        scores.append(held(part))
        rows.append(row)
        cols.append(col)
    part, row_joint, sent = call(
        functools.partial(end_kernel, scale),
        (kept(2 * LANES), f32(16, LANES), f32(GROUP * GROUP, LANES)),
        *both,
        *[blocks[slot] for slot in CALLS[-1]],
        *rows,
        *cols,
        flops=4 * LANES * 2048 * 1024,
        exps=4 * LANES * 2048,
        scratch=[pltpu.VMEM((GROUP, LANES), jnp.float32), pltpu.VMEM((16, LANES), jnp.float32)],
    )
    scores.append(held(part))
    received = exchange(sent)
    joint, col_norm = call(
        functools.partial(row_best_kernel, scale),
        (f32(32, LANES), f32(GROUP, LANES)),
        *scores,
        received,
        row_joint,
        flops=2 * 1024 * 2048,
    )
    joint = call(core_kernel, f32(32, LANES), joint, move(joint, to_core))
    sent = call(join_kernel, f32(ZS * 32, LANES), joint, move(joint, to_far))
    along_z = [[2 * z + k for z in range(ZS)] for k in range(2)]
    received = lax.all_to_all(sent, "wide", 0, 0, axis_index_groups=along_z, tiled=True)
    sent, row_best = call(
        functools.partial(col_best_kernel, scale),
        (f32(GROUP, LANES), pltpu.VMEM((8, LANES), jnp.float32)),
        *scores,
        received,
        col_norm,
        flops=2 * 1024 * 2048,
    )
    received = exchange(sent)
    row_best, col_best = call(
        last_kernel, (f32(8, LANES), f32(1, LANES)), received, held(row_best)
    )
    return row_best.reshape(1024), col_best.reshape(LANES)


def solution(mesh):
    return jax.shard_map(
        body,
        mesh=mesh,
        in_specs=(P("narrow", None), P(("wide", "narrow"), None)),
        out_specs=(P("narrow"), P(("wide", "narrow"))),
        check_vma=False,
    )
```

```python
import functools
import math

import jax
import jax.numpy as jnp
from jax import lax
from jax.experimental import pallas as pl
from jax.experimental.pallas import tpu as pltpu
from jax.sharding import PartitionSpec as P

XS, YS, ZS, CORES = 4, 4, 8, 2
BOTH = ("wide", "narrow")
GROUP = 8
LANES = 128


def device_index(z, y, x, core):
    y, x, z = y % YS, x % XS, z % ZS
    return (z * 2 + y // 2) * 16 + (y % 2) * 8 + x * 2 + core


def places():
    for z in range(ZS):
        for y in range(YS):
            for x in range(XS):
                for core in range(CORES):
                    yield z, y, x, core


def partner(y, core):
    return y ^ 1 if core == 0 else 3 - y


def move(value, where):
    pairs = [(device_index(*place), device_index(*where(*place))) for place in places()]
    return lax.ppermute(value, BOTH, pairs)


def ahead(z, y, x, core):
    return z, y, x + 1 - 2 * core, core


def behind(z, y, x, core):
    return z, y, x - 1 + 2 * core, core


def across(z, y, x, core):
    return z, partner(y, core), x, core


def ahead_across(z, y, x, core):
    return z, partner(y, core), x + 1 - 2 * core, core


def to_core(z, y, x, core):
    return z, y, x, 1 - core


def to_far(z, y, x, core):
    return z, y + 2, x, core


def column_groups():
    groups = []
    for z in range(ZS):
        for core in range(CORES):
            for y in (0, 2):
                rows = (y, partner(y, core))
                groups.append([device_index(z, row, x, core) for row in rows for x in range(XS)])
    return groups


def vmem():
    return pl.BlockSpec(memory_space=pltpu.VMEM)


def after(values):
    return lax.optimization_barrier(values)


def held(value):
    return pltpu.with_memory_space_constraint(value, pltpu.VMEM)


def call(kernel, out_shape, *operands, flops=0, exps=0, scratch=(), far=(), limit=24):
    moved = sum(math.prod(o.shape) * o.dtype.itemsize for o in operands)
    return pl.pallas_call(
        kernel,
        out_shape=out_shape,
        in_specs=[pl.BlockSpec(memory_space=pltpu.HBM) if k in far else vmem() for k in range(len(operands))],
        out_specs=jax.tree.map(lambda _: vmem(), out_shape),
        scratch_shapes=list(scratch),
        cost_estimate=pl.CostEstimate(flops=flops, bytes_accessed=moved, transcendentals=exps),
        compiler_params=pltpu.CompilerParams(vmem_limit_bytes=limit * 1024 * 1024),
    )(*operands)


def f32(*shape):
    return jax.ShapeDtypeStruct(shape, jnp.float32)


def eye():
    row = lax.broadcasted_iota(jnp.int32, (LANES, LANES), 0)
    return row == lax.broadcasted_iota(jnp.int32, (LANES, LANES), 1)


def as_row(column):
    return jnp.sum(jnp.where(eye(), column, 0.0), axis=0, keepdims=True)


def as_column(row):
    return jnp.sum(jnp.where(eye(), row, 0.0), axis=1, keepdims=True)


def own_place():
    narrow = lax.axis_index("narrow")
    return narrow // 8, (narrow // 2) % 4, narrow % 2


def owner(place, slot):
    y_lo, x, core = place
    dx, dy = slot
    return ((y_lo + dy) % 2) * 4 + (x + 4 + dx * (1 - 2 * core)) % 4


CALLS = (((0, 0), (0, 1)), ((3, 0), (1, 0)), ((3, 1), (2, 0), (2, 1)), ((1, 1),))
SLOTS = tuple((call, k, slot) for call, slots in enumerate(CALLS) for k, slot in enumerate(slots))


def products(scale, s0, s1, targets, scores, row_part):
    count = targets.shape[0]
    rate = scale / math.log(2.0)
    running = None
    for i in range(8):
        source = (s0 if i < 4 else s1)[pl.ds((i % 4) * 256, 256), :]
        part = lax.dot_general(
            targets, source, (((1,), (1,)), ((), ())), preferred_element_type=jnp.float32
        )
        scores[:, pl.ds(i * 256, 256)] = part
        top = jnp.max(part, axis=0, keepdims=True)
        total = jnp.sum(jnp.exp2((part - top) * rate), axis=0, keepdims=True)
        result = top * scale + jnp.log(total)
        row_part[pl.ds(2 * i, 1), :] = result[:, :LANES]
        row_part[pl.ds(2 * i + 1, 1), :] = result[:, LANES:]
        top = jnp.maximum(part[:, :LANES], part[:, LANES:])
        running = top if running is None else jnp.maximum(running, top)
    top = jnp.max(running, axis=1, keepdims=True)
    total = jnp.zeros((count, LANES), jnp.float32)
    for j in range(16):
        total += jnp.exp2((scores[:, pl.ds(j * LANES, LANES)] - top) * rate)
    result = top * scale + jnp.log(jnp.sum(total, axis=1, keepdims=True))
    return [as_row(result[k : k + LANES]) for k in range(0, count, LANES)]


def bring_kernel(sources, targets, sources_here, targets_here, sems):
    copies = [pltpu.make_async_copy(targets, targets_here, sems.at[0])]
    for i in range(8):
        rows = pl.ds(i * 128, 128)
        copies.append(pltpu.make_async_copy(sources.at[rows], sources_here.at[rows], sems.at[i + 1]))
    for copy in copies:
        copy.start()
    for copy in copies:
        copy.wait()


def some_kernel(scale, s0, s1, *refs):
    blocks, (scores, row_part, col_part) = refs[:-3], refs[-3:]
    targets = jnp.concatenate([block[...] for block in blocks], axis=0)
    for k, row in enumerate(products(scale, s0, s1, targets, scores, row_part)):
        col_part[pl.ds(k, 1), :] = row


def end_kernel(scale, s0, s1, ta, *refs):
    rows, cols = refs[:3], refs[3:6]
    scores, joint, sent, scratch, last = refs[6:]
    ends = products(scale, s0, s1, ta[...], scores, last)
    joint[...] = log_sum([row[...] for row in rows] + [last[...]])
    place = own_place()
    for call, k, slot in SLOTS:
        row = ends[k] if call == 3 else cols[call][pl.ds(k, 1), :]
        scratch[pl.ds(owner(place, slot), 1), :] = row
    whole = scratch[...]
    for e in range(GROUP):
        sent[pl.ds(e * GROUP, GROUP), :] = whole


def log_sum(parts):
    top = functools.reduce(jnp.maximum, parts)
    return top + jnp.log(sum(jnp.exp(part - top) for part in parts))


def row_best_kernel(scale, a0, a1, a2, a3, received, row_joint, rows, col_norm):
    norm = log_sum([received[pl.ds(e * GROUP, GROUP), :] for e in range(GROUP)])
    col_norm[...] = norm
    place = own_place()
    half = 0.5 / scale
    best = [None] * 16
    for call, k, slot in SLOTS:
        column = as_column(col_norm[pl.ds(owner(place, slot), 1), :]) * half
        column = jnp.broadcast_to(column, (LANES, LANES))
        block = (a0, a1, a2, a3)[call]
        for j in range(16):
            part = block[pl.ds(k * LANES, LANES), pl.ds(j * LANES, LANES)] - column
            part = functools.reduce(jnp.maximum, [part[8 * q : 8 * q + 8] for q in range(16)])
            best[j] = part if best[j] is None else jnp.maximum(best[j], part)
    rows[:16] = row_joint[...]
    for j in range(16):
        rows[pl.ds(16 + j, 1), :] = jnp.max(best[j], axis=0, keepdims=True) * scale


def core_kernel(rows, core, joint):
    joint[:8] = log_sum([rows[:8], core[8:16]])
    joint[8:16] = log_sum([rows[8:16], core[:8]])
    joint[16:] = jnp.maximum(rows[16:24], core[24:])


def join_kernel(rows, far, sent):
    norm = log_sum([rows[:16], far[:16]])
    best = jnp.maximum(rows[16:], far[16:])
    for e in range(ZS):
        sent[pl.ds(e * 24, 16), :] = norm
        sent[pl.ds(e * 24 + 16, 8), :] = best


def col_best_kernel(scale, a0, a1, a2, a3, received, col_norm, sent, row_best):
    parts = [received[pl.ds(e * 24, 16), :] for e in range(ZS)]
    row_norm = log_sum(parts)
    best = functools.reduce(jnp.maximum, [received[pl.ds(e * 24 + 16, 8), :] for e in range(ZS)])
    row_best[...] = best - 0.5 * row_norm[:8]
    place = own_place()
    norms = row_norm * (0.5 / scale)
    for call, k, slot in SLOTS:
        block = (a0, a1, a2, a3)[call]
        best = None
        for j in range(16):
            part = block[pl.ds(k * LANES, LANES), pl.ds(j * LANES, LANES)] - norms[j : j + 1, :]
            best = part if best is None else jnp.maximum(best, part)
        best = as_row(jnp.max(best, axis=1, keepdims=True)) * scale
        position = owner(place, slot)
        sent[pl.ds(position, 1), :] = best - 0.5 * col_norm[pl.ds(position, 1), :]


def last_kernel(received, row_best_held, row_best, col_best):
    row_best[...] = row_best_held[...]
    col_best[...] = jnp.max(received[...], axis=0, keepdims=True)


def body(sources, targets):
    scale = 1.0 / math.sqrt(sources.shape[1])
    groups = column_groups()

    def exchange(value):
        return lax.all_to_all(value, BOTH, 0, 0, axis_index_groups=groups, tiled=True)

    def kept(rows):
        return pltpu.VMEM((rows, 2048), jnp.float32)

    blocks = {}
    blocks[3, 0] = move(targets, ahead)
    blocks[0, 1] = move(targets, across)
    other = held(move(sources, to_core))
    sources, blocks[0, 0] = call(
        bring_kernel,
        (pltpu.VMEM((1024, 1024), jnp.bfloat16), pltpu.VMEM((LANES, 1024), jnp.bfloat16)),
        pltpu.with_memory_space_constraint(sources, pltpu.HBM),
        pltpu.with_memory_space_constraint(targets, pltpu.HBM),
        far=(0, 1),
        scratch=[pltpu.SemaphoreType.DMA((9,))],
    )
    blocks[1, 0] = move(blocks[0, 0], behind)
    blocks[3, 0], blocks[0, 0] = after((blocks[3, 0], blocks[0, 0]))
    blocks[2, 1] = move(blocks[3, 0], ahead_across)
    blocks[2, 0] = move(blocks[3, 0], ahead)
    blocks[3, 1] = move(blocks[3, 0], across)
    both = (held(sources), other)

    scores, rows, cols = [], [], []
    for n, slots in enumerate(CALLS[:-1]):
        count = len(slots) * LANES
        if n == 1:
            blocks[1, 0], rows[0] = after((blocks[1, 0], rows[0]))
            blocks[1, 1] = move(blocks[1, 0], across)
        part, row, col = call(
            functools.partial(some_kernel, scale),
            (kept(count), f32(16, LANES), f32(len(slots), LANES)),
            *both,
            *[blocks[slot] for slot in slots],
            flops=2 * count * 2048 * 1024,
            exps=2 * count * 2048,
        )
        scores.append(held(part))
        rows.append(row)
        cols.append(col)
    part, row_joint, sent = call(
        functools.partial(end_kernel, scale),
        (kept(LANES), f32(16, LANES), f32(GROUP * GROUP, LANES)),
        *both,
        *[blocks[slot] for slot in CALLS[-1]],
        *rows,
        *cols,
        flops=2 * LANES * 2048 * 1024,
        exps=2 * LANES * 2048,
        scratch=[pltpu.VMEM((GROUP, LANES), jnp.float32), pltpu.VMEM((16, LANES), jnp.float32)],
    )
    scores.append(held(part))
    received = exchange(sent)
    joint, col_norm = call(
        functools.partial(row_best_kernel, scale),
        (f32(32, LANES), f32(GROUP, LANES)),
        *scores,
        received,
        row_joint,
        flops=2 * 1024 * 2048,
    )
    joint = call(core_kernel, f32(24, LANES), joint, move(joint, to_core))
    sent = call(join_kernel, f32(ZS * 24, LANES), joint, move(joint, to_far))
    along_z = [[2 * z + k for z in range(ZS)] for k in range(2)]
    received = lax.all_to_all(sent, "wide", 0, 0, axis_index_groups=along_z, tiled=True)
    sent, row_best = call(
        functools.partial(col_best_kernel, scale),
        (f32(GROUP, LANES), pltpu.VMEM((8, LANES), jnp.float32)),
        *scores,
        received,
        col_norm,
        flops=2 * 1024 * 2048,
    )
    received = exchange(sent)
    row_best, col_best = call(
        last_kernel, (f32(8, LANES), f32(1, LANES)), received, held(row_best)
    )
    return row_best.reshape(1024), col_best.reshape(LANES)


def solution(mesh):
    return jax.shard_map(
        body,
        mesh=mesh,
        in_specs=(P("narrow", None), P(("wide", "narrow"), None)),
        out_specs=(P("narrow"), P(("wide", "narrow"))),
        check_vma=False,
    )
```

```python
import functools
import math

import jax
import jax.numpy as jnp
from jax import lax
from jax.experimental import pallas as pl
from jax.experimental.pallas import tpu as pltpu
from jax.sharding import PartitionSpec as P

XS, YS, ZS, CORES = 4, 4, 8, 2
BOTH = ("wide", "narrow")
GROUP = 8
LANES = 128


def device_index(z, y, x, core):
    y, x, z = y % YS, x % XS, z % ZS
    return (z * 2 + y // 2) * 16 + (y % 2) * 8 + x * 2 + core


def places():
    for z in range(ZS):
        for y in range(YS):
            for x in range(XS):
                for core in range(CORES):
                    yield z, y, x, core


def partner(y, core):
    return y ^ 1 if core == 0 else 3 - y


def move(value, where):
    pairs = [(device_index(*place), device_index(*where(*place))) for place in places()]
    return lax.ppermute(value, BOTH, pairs)


def ahead(z, y, x, core):
    return z, y, x + 1 - 2 * core, core


def behind(z, y, x, core):
    return z, y, x - 1 + 2 * core, core


def across(z, y, x, core):
    return z, partner(y, core), x, core


def ahead_across(z, y, x, core):
    return z, partner(y, core), x + 1 - 2 * core, core


def to_core(z, y, x, core):
    return z, y, x, 1 - core


def to_far(z, y, x, core):
    return z, y + 2, x, core


def column_groups():
    groups = []
    for z in range(ZS):
        for core in range(CORES):
            for y in (0, 2):
                rows = (y, partner(y, core))
                groups.append([device_index(z, row, x, core) for row in rows for x in range(XS)])
    return groups


def vmem():
    return pl.BlockSpec(memory_space=pltpu.VMEM)


def after(values):
    return lax.optimization_barrier(values)


def held(value):
    return pltpu.with_memory_space_constraint(value, pltpu.VMEM)


def call(kernel, out_shape, *operands, flops=0, exps=0, scratch=(), far=(), limit=24):
    moved = sum(math.prod(o.shape) * o.dtype.itemsize for o in operands)
    return pl.pallas_call(
        kernel,
        out_shape=out_shape,
        in_specs=[pl.BlockSpec(memory_space=pltpu.HBM) if k in far else vmem() for k in range(len(operands))],
        out_specs=jax.tree.map(lambda _: vmem(), out_shape),
        scratch_shapes=list(scratch),
        cost_estimate=pl.CostEstimate(flops=flops, bytes_accessed=moved, transcendentals=exps),
        compiler_params=pltpu.CompilerParams(vmem_limit_bytes=limit * 1024 * 1024),
    )(*operands)


def f32(*shape):
    return jax.ShapeDtypeStruct(shape, jnp.float32)


def eye():
    row = lax.broadcasted_iota(jnp.int32, (LANES, LANES), 0)
    return row == lax.broadcasted_iota(jnp.int32, (LANES, LANES), 1)


def as_row(column):
    return jnp.sum(jnp.where(eye(), column, 0.0), axis=0, keepdims=True)


def as_column(row):
    return jnp.sum(jnp.where(eye(), row, 0.0), axis=1, keepdims=True)


def own_place():
    narrow = lax.axis_index("narrow")
    return narrow // 8, (narrow // 2) % 4, narrow % 2


def owner(place, slot):
    y_lo, x, core = place
    dx, dy = slot
    return ((y_lo + dy) % 2) * 4 + (x + 4 + dx * (1 - 2 * core)) % 4


CALLS = (((0, 0), (0, 1)), ((3, 0), (1, 0)), ((2, 1), (3, 1), (2, 0)), ((1, 1),))
SLOTS = tuple((call, k, slot) for call, slots in enumerate(CALLS) for k, slot in enumerate(slots))


def products(scale, s0, s1, targets, scores, row_part):
    count = targets.shape[0]
    rate = scale / math.log(2.0)
    running = None
    for i in range(8):
        source = (s0 if i < 4 else s1)[pl.ds((i % 4) * 256, 256), :]
        part = lax.dot_general(
            targets, source, (((1,), (1,)), ((), ())), preferred_element_type=jnp.float32
        )
        scores[:, pl.ds(i * 256, 256)] = part
        top = jnp.max(part, axis=0, keepdims=True)
        total = jnp.sum(jnp.exp2((part - top) * rate), axis=0, keepdims=True)
        result = top * scale + jnp.log(total)
        row_part[pl.ds(2 * i, 1), :] = result[:, :LANES]
        row_part[pl.ds(2 * i + 1, 1), :] = result[:, LANES:]
        top = jnp.maximum(part[:, :LANES], part[:, LANES:])
        running = top if running is None else jnp.maximum(running, top)
    top = jnp.max(running, axis=1, keepdims=True)
    total = jnp.zeros((count, LANES), jnp.float32)
    for j in range(16):
        total += jnp.exp2((scores[:, pl.ds(j * LANES, LANES)] - top) * rate)
    result = top * scale + jnp.log(jnp.sum(total, axis=1, keepdims=True))
    return [as_row(result[k : k + LANES]) for k in range(0, count, LANES)]


def bring_kernel(sources, targets, sources_here, targets_here, sems):
    copies = [pltpu.make_async_copy(targets, targets_here, sems.at[0])]
    for i in range(8):
        rows = pl.ds(i * 128, 128)
        copies.append(pltpu.make_async_copy(sources.at[rows], sources_here.at[rows], sems.at[i + 1]))
    for copy in copies:
        copy.start()
    for copy in copies:
        copy.wait()


def some_kernel(scale, s0, s1, *refs):
    blocks, (scores, row_part, col_part) = refs[:-3], refs[-3:]
    targets = jnp.concatenate([block[...] for block in blocks], axis=0)
    for k, row in enumerate(products(scale, s0, s1, targets, scores, row_part)):
        col_part[pl.ds(k, 1), :] = row


def end_kernel(scale, s0, s1, ta, *refs):
    rows, cols = refs[:3], refs[3:6]
    scores, joint, sent, scratch, last = refs[6:]
    ends = products(scale, s0, s1, ta[...], scores, last)
    joint[...] = log_sum([row[...] for row in rows] + [last[...]])
    place = own_place()
    for call, k, slot in SLOTS:
        row = ends[k] if call == 3 else cols[call][pl.ds(k, 1), :]
        scratch[pl.ds(owner(place, slot), 1), :] = row
    whole = scratch[...]
    for e in range(GROUP):
        sent[pl.ds(e * GROUP, GROUP), :] = whole


def log_sum(parts):
    top = functools.reduce(jnp.maximum, parts)
    return top + jnp.log(sum(jnp.exp(part - top) for part in parts))


def row_best_kernel(scale, a0, a1, a2, a3, received, row_joint, rows, col_norm):
    norm = log_sum([received[pl.ds(e * GROUP, GROUP), :] for e in range(GROUP)])
    col_norm[...] = norm
    place = own_place()
    half = 0.5 / scale
    best = [None] * 16
    for call, k, slot in SLOTS:
        column = as_column(col_norm[pl.ds(owner(place, slot), 1), :]) * half
        column = jnp.broadcast_to(column, (LANES, LANES))
        block = (a0, a1, a2, a3)[call]
        for j in range(16):
            part = block[pl.ds(k * LANES, LANES), pl.ds(j * LANES, LANES)] - column
            part = functools.reduce(jnp.maximum, [part[8 * q : 8 * q + 8] for q in range(16)])
            best[j] = part if best[j] is None else jnp.maximum(best[j], part)
    rows[:16] = row_joint[...]
    for j in range(16):
        rows[pl.ds(16 + j, 1), :] = jnp.max(best[j], axis=0, keepdims=True) * scale


def core_kernel(rows, core, joint):
    joint[:8] = log_sum([rows[:8], core[8:16]])
    joint[8:16] = log_sum([rows[8:16], core[:8]])
    joint[16:] = jnp.maximum(rows[16:24], core[24:])


def join_kernel(rows, far, sent):
    norm = log_sum([rows[:16], far[:16]])
    best = jnp.maximum(rows[16:], far[16:])
    for e in range(ZS):
        sent[pl.ds(e * 24, 16), :] = norm
        sent[pl.ds(e * 24 + 16, 8), :] = best


def col_best_kernel(scale, a0, a1, a2, a3, received, col_norm, sent, row_best):
    parts = [received[pl.ds(e * 24, 16), :] for e in range(ZS)]
    row_norm = log_sum(parts)
    best = functools.reduce(jnp.maximum, [received[pl.ds(e * 24 + 16, 8), :] for e in range(ZS)])
    row_best[...] = best - 0.5 * row_norm[:8]
    place = own_place()
    norms = row_norm * (0.5 / scale)
    for call, k, slot in SLOTS:
        block = (a0, a1, a2, a3)[call]
        best = None
        for j in range(16):
            part = block[pl.ds(k * LANES, LANES), pl.ds(j * LANES, LANES)] - norms[j : j + 1, :]
            best = part if best is None else jnp.maximum(best, part)
        best = as_row(jnp.max(best, axis=1, keepdims=True)) * scale
        position = owner(place, slot)
        sent[pl.ds(position, 1), :] = best - 0.5 * col_norm[pl.ds(position, 1), :]


def last_kernel(received, row_best_held, row_best, col_best):
    row_best[...] = row_best_held[...]
    col_best[...] = jnp.max(received[...], axis=0, keepdims=True)


def body(sources, targets):
    scale = 1.0 / math.sqrt(sources.shape[1])
    groups = column_groups()

    def exchange(value):
        return lax.all_to_all(value, BOTH, 0, 0, axis_index_groups=groups, tiled=True)

    def kept(rows):
        return pltpu.VMEM((rows, 2048), jnp.float32)

    blocks = {}
    blocks[3, 0] = move(targets, ahead)
    blocks[0, 1] = move(targets, across)
    other = held(move(sources, to_core))
    sources, blocks[0, 0] = call(
        bring_kernel,
        (pltpu.VMEM((1024, 1024), jnp.bfloat16), pltpu.VMEM((LANES, 1024), jnp.bfloat16)),
        pltpu.with_memory_space_constraint(sources, pltpu.HBM),
        pltpu.with_memory_space_constraint(targets, pltpu.HBM),
        far=(0, 1),
        scratch=[pltpu.SemaphoreType.DMA((9,))],
    )
    blocks[1, 0] = move(blocks[0, 0], behind)
    blocks[3, 0], blocks[0, 0] = after((blocks[3, 0], blocks[0, 0]))
    blocks[3, 1] = move(blocks[3, 0], across)
    blocks[2, 0] = move(blocks[3, 0], ahead)
    blocks[2, 1] = move(blocks[3, 0], ahead_across)
    both = (held(sources), other)

    scores, rows, cols = [], [], []
    for n, slots in enumerate(CALLS[:-1]):
        count = len(slots) * LANES
        if n == 1:
            blocks[1, 0], rows[0] = after((blocks[1, 0], rows[0]))
            blocks[1, 1] = move(blocks[1, 0], across)
        part, row, col = call(
            functools.partial(some_kernel, scale),
            (kept(count), f32(16, LANES), f32(len(slots), LANES)),
            *both,
            *[blocks[slot] for slot in slots],
            flops=2 * count * 2048 * 1024,
            exps=2 * count * 2048,
        )
        scores.append(held(part))
        rows.append(row)
        cols.append(col)
    part, row_joint, sent = call(
        functools.partial(end_kernel, scale),
        (kept(LANES), f32(16, LANES), f32(GROUP * GROUP, LANES)),
        *both,
        *[blocks[slot] for slot in CALLS[-1]],
        *rows,
        *cols,
        flops=2 * LANES * 2048 * 1024,
        exps=2 * LANES * 2048,
        scratch=[pltpu.VMEM((GROUP, LANES), jnp.float32), pltpu.VMEM((16, LANES), jnp.float32)],
    )
    scores.append(held(part))
    received = exchange(sent)
    joint, col_norm = call(
        functools.partial(row_best_kernel, scale),
        (f32(32, LANES), f32(GROUP, LANES)),
        *scores,
        received,
        row_joint,
        flops=2 * 1024 * 2048,
    )
    joint = call(core_kernel, f32(24, LANES), joint, move(joint, to_core))
    sent = call(join_kernel, f32(ZS * 24, LANES), joint, move(joint, to_far))
    along_z = [[2 * z + k for z in range(ZS)] for k in range(2)]
    received = lax.all_to_all(sent, "wide", 0, 0, axis_index_groups=along_z, tiled=True)
    sent, row_best = call(
        functools.partial(col_best_kernel, scale),
        (f32(GROUP, LANES), pltpu.VMEM((8, LANES), jnp.float32)),
        *scores,
        received,
        col_norm,
        flops=2 * 1024 * 2048,
    )
    received = exchange(sent)
    row_best, col_best = call(
        last_kernel, (f32(8, LANES), f32(1, LANES)), received, held(row_best)
    )
    return row_best.reshape(1024), col_best.reshape(LANES)


def solution(mesh):
    return jax.shard_map(
        body,
        mesh=mesh,
        in_specs=(P("narrow", None), P(("wide", "narrow"), None)),
        out_specs=(P("narrow"), P(("wide", "narrow"))),
        check_vma=False,
    )
```

```python
import functools
import math

import jax
import jax.numpy as jnp
from jax import lax
from jax.experimental import pallas as pl
from jax.experimental.pallas import tpu as pltpu
from jax.sharding import PartitionSpec as P

XS, YS, ZS, CORES = 4, 4, 8, 2
BOTH = ("wide", "narrow")
GROUP = 8
LANES = 128


def device_index(z, y, x, core):
    y, x, z = y % YS, x % XS, z % ZS
    return (z * 2 + y // 2) * 16 + (y % 2) * 8 + x * 2 + core


def places():
    for z in range(ZS):
        for y in range(YS):
            for x in range(XS):
                for core in range(CORES):
                    yield z, y, x, core


def partner(y, core):
    return y ^ 1 if core == 0 else 3 - y


def move(value, where):
    pairs = [(device_index(*place), device_index(*where(*place))) for place in places()]
    return lax.ppermute(value, BOTH, pairs)


def ahead(z, y, x, core):
    return z, y, x + 1 - 2 * core, core


def behind(z, y, x, core):
    return z, y, x - 1 + 2 * core, core


def across(z, y, x, core):
    return z, partner(y, core), x, core


def ahead_across(z, y, x, core):
    return z, partner(y, core), x + 1 - 2 * core, core


def to_core(z, y, x, core):
    return z, y, x, 1 - core


def to_far(z, y, x, core):
    return z, y + 2, x, core


def column_groups():
    groups = []
    for z in range(ZS):
        for core in range(CORES):
            for y in (0, 2):
                rows = (y, partner(y, core))
                groups.append([device_index(z, row, x, core) for row in rows for x in range(XS)])
    return groups


def vmem():
    return pl.BlockSpec(memory_space=pltpu.VMEM)


def after(values):
    return lax.optimization_barrier(values)


def held(value):
    return pltpu.with_memory_space_constraint(value, pltpu.VMEM)


def call(kernel, out_shape, *operands, flops=0, exps=0, scratch=(), far=(), limit=24):
    moved = sum(math.prod(o.shape) * o.dtype.itemsize for o in operands)
    return pl.pallas_call(
        kernel,
        out_shape=out_shape,
        in_specs=[pl.BlockSpec(memory_space=pltpu.HBM) if k in far else vmem() for k in range(len(operands))],
        out_specs=jax.tree.map(lambda _: vmem(), out_shape),
        scratch_shapes=list(scratch),
        cost_estimate=pl.CostEstimate(flops=flops, bytes_accessed=moved, transcendentals=exps),
        compiler_params=pltpu.CompilerParams(vmem_limit_bytes=limit * 1024 * 1024),
    )(*operands)


def f32(*shape):
    return jax.ShapeDtypeStruct(shape, jnp.float32)


def eye():
    row = lax.broadcasted_iota(jnp.int32, (LANES, LANES), 0)
    return row == lax.broadcasted_iota(jnp.int32, (LANES, LANES), 1)


def as_row(column):
    return jnp.sum(jnp.where(eye(), column, 0.0), axis=0, keepdims=True)


def as_column(row):
    return jnp.sum(jnp.where(eye(), row, 0.0), axis=1, keepdims=True)


def own_place():
    narrow = lax.axis_index("narrow")
    return narrow // 8, (narrow // 2) % 4, narrow % 2


def owner(place, slot):
    y_lo, x, core = place
    dx, dy = slot
    return ((y_lo + dy) % 2) * 4 + (x + 4 + dx * (1 - 2 * core)) % 4


CALLS = (((0, 0), (0, 1)), ((3, 0), (1, 0)), ((2, 1), (3, 1), (2, 0)), ((1, 1),))
SLOTS = tuple((call, k, slot) for call, slots in enumerate(CALLS) for k, slot in enumerate(slots))


def products(scale, s0, s1, targets, scores, row_part):
    count = targets.shape[0]
    rate = scale / math.log(2.0)
    running = None
    for i in range(8):
        source = (s0 if i < 4 else s1)[pl.ds((i % 4) * 256, 256), :]
        part = lax.dot_general(
            targets, source, (((1,), (1,)), ((), ())), preferred_element_type=jnp.float32
        )
        scores[:, pl.ds(i * 256, 256)] = part
        top = jnp.max(part, axis=0, keepdims=True)
        total = jnp.sum(jnp.exp2((part - top) * rate), axis=0, keepdims=True)
        result = top * scale + jnp.log(total)
        row_part[pl.ds(2 * i, 1), :] = result[:, :LANES]
        row_part[pl.ds(2 * i + 1, 1), :] = result[:, LANES:]
        top = jnp.maximum(part[:, :LANES], part[:, LANES:])
        running = top if running is None else jnp.maximum(running, top)
    top = jnp.max(running, axis=1, keepdims=True)
    total = jnp.zeros((count, LANES), jnp.float32)
    for j in range(16):
        total += jnp.exp2((scores[:, pl.ds(j * LANES, LANES)] - top) * rate)
    result = top * scale + jnp.log(jnp.sum(total, axis=1, keepdims=True))
    return [as_row(result[k : k + LANES]) for k in range(0, count, LANES)]


def bring_kernel(sources, targets, sources_here, targets_here, sems):
    copies = [pltpu.make_async_copy(targets, targets_here, sems.at[0])]
    for i in range(8):
        rows = pl.ds(i * 128, 128)
        copies.append(pltpu.make_async_copy(sources.at[rows], sources_here.at[rows], sems.at[i + 1]))
    for copy in copies:
        copy.start()
    for copy in copies:
        copy.wait()


def some_kernel(scale, s0, s1, *refs):
    blocks, (scores, row_part, col_part) = refs[:-3], refs[-3:]
    targets = jnp.concatenate([block[...] for block in blocks], axis=0)
    for k, row in enumerate(products(scale, s0, s1, targets, scores, row_part)):
        col_part[pl.ds(k, 1), :] = row


def end_kernel(scale, s0, s1, ta, *refs):
    rows, cols = refs[:3], refs[3:6]
    scores, joint, sent, scratch, last = refs[6:]
    ends = products(scale, s0, s1, ta[...], scores, last)
    joint[...] = log_sum([row[...] for row in rows] + [last[...]])
    place = own_place()
    for call, k, slot in SLOTS:
        row = ends[k] if call == 3 else cols[call][pl.ds(k, 1), :]
        scratch[pl.ds(owner(place, slot), 1), :] = row
    whole = scratch[...]
    for e in range(GROUP):
        sent[pl.ds(e * GROUP, GROUP), :] = whole


def log_sum(parts):
    top = functools.reduce(jnp.maximum, parts)
    return top + jnp.log(sum(jnp.exp(part - top) for part in parts))


def row_best_kernel(scale, a0, a1, a2, a3, received, row_joint, rows, col_norm):
    norm = log_sum([received[pl.ds(e * GROUP, GROUP), :] for e in range(GROUP)])
    col_norm[...] = norm
    place = own_place()
    half = 0.5 / scale
    best = [None] * 16
    for call, k, slot in SLOTS:
        column = as_column(col_norm[pl.ds(owner(place, slot), 1), :]) * half
        column = jnp.broadcast_to(column, (LANES, LANES))
        block = (a0, a1, a2, a3)[call]
        for j in range(16):
            part = block[pl.ds(k * LANES, LANES), pl.ds(j * LANES, LANES)] - column
            part = functools.reduce(jnp.maximum, [part[8 * q : 8 * q + 8] for q in range(16)])
            best[j] = part if best[j] is None else jnp.maximum(best[j], part)
    rows[:16] = row_joint[...]
    for j in range(16):
        rows[pl.ds(16 + j, 1), :] = jnp.max(best[j], axis=0, keepdims=True) * scale


def core_kernel(rows, core, joint):
    joint[:8] = log_sum([rows[:8], core[8:16]])
    joint[8:16] = log_sum([rows[8:16], core[:8]])
    joint[16:] = jnp.maximum(rows[16:24], core[24:])


def join_kernel(rows, far, sent):
    norm = log_sum([rows[:16], far[:16]])
    best = jnp.maximum(rows[16:], far[16:])
    for e in range(ZS):
        sent[pl.ds(e * 24, 16), :] = norm
        sent[pl.ds(e * 24 + 16, 8), :] = best


def col_best_kernel(scale, a0, a1, a2, a3, received, col_norm, sent, row_best):
    parts = [received[pl.ds(e * 24, 16), :] for e in range(ZS)]
    row_norm = log_sum(parts)
    best = functools.reduce(jnp.maximum, [received[pl.ds(e * 24 + 16, 8), :] for e in range(ZS)])
    row_best[...] = best - 0.5 * row_norm[:8]
    place = own_place()
    norms = row_norm * (0.5 / scale)
    for call, k, slot in SLOTS:
        block = (a0, a1, a2, a3)[call]
        best = None
        for j in range(16):
            part = block[pl.ds(k * LANES, LANES), pl.ds(j * LANES, LANES)] - norms[j : j + 1, :]
            best = part if best is None else jnp.maximum(best, part)
        best = as_row(jnp.max(best, axis=1, keepdims=True)) * scale
        position = owner(place, slot)
        sent[pl.ds(position, 1), :] = best - 0.5 * col_norm[pl.ds(position, 1), :]


def last_kernel(received, col_best):
    col_best[...] = jnp.max(received[...], axis=0, keepdims=True)


def body(sources, targets):
    scale = 1.0 / math.sqrt(sources.shape[1])
    groups = column_groups()

    def exchange(value):
        return lax.all_to_all(value, BOTH, 0, 0, axis_index_groups=groups, tiled=True)

    def kept(rows):
        return pltpu.VMEM((rows, 2048), jnp.float32)

    blocks = {}
    blocks[3, 0] = move(targets, ahead)
    blocks[0, 1] = move(targets, across)
    other = held(move(sources, to_core))
    sources, blocks[0, 0] = call(
        bring_kernel,
        (pltpu.VMEM((1024, 1024), jnp.bfloat16), pltpu.VMEM((LANES, 1024), jnp.bfloat16)),
        pltpu.with_memory_space_constraint(sources, pltpu.HBM),
        pltpu.with_memory_space_constraint(targets, pltpu.HBM),
        far=(0, 1),
        scratch=[pltpu.SemaphoreType.DMA((9,))],
    )
    blocks[1, 0] = move(blocks[0, 0], behind)
    blocks[3, 0], blocks[0, 0] = after((blocks[3, 0], blocks[0, 0]))
    blocks[3, 1] = move(blocks[3, 0], across)
    blocks[2, 0] = move(blocks[3, 0], ahead)
    blocks[2, 1] = move(blocks[3, 0], ahead_across)
    both = (held(sources), other)

    scores, rows, cols = [], [], []
    for n, slots in enumerate(CALLS[:-1]):
        count = len(slots) * LANES
        if n == 1:
            blocks[1, 0], rows[0] = after((blocks[1, 0], rows[0]))
            blocks[1, 1] = move(blocks[1, 0], across)
        part, row, col = call(
            functools.partial(some_kernel, scale),
            (kept(count), f32(16, LANES), f32(len(slots), LANES)),
            *both,
            *[blocks[slot] for slot in slots],
            flops=2 * count * 2048 * 1024,
            exps=2 * count * 2048,
        )
        scores.append(held(part))
        rows.append(row)
        cols.append(col)
    part, row_joint, sent = call(
        functools.partial(end_kernel, scale),
        (kept(LANES), f32(16, LANES), f32(GROUP * GROUP, LANES)),
        *both,
        *[blocks[slot] for slot in CALLS[-1]],
        *rows,
        *cols,
        flops=2 * LANES * 2048 * 1024,
        exps=2 * LANES * 2048,
        scratch=[pltpu.VMEM((GROUP, LANES), jnp.float32), pltpu.VMEM((16, LANES), jnp.float32)],
    )
    scores.append(held(part))
    received = exchange(sent)
    joint, col_norm = call(
        functools.partial(row_best_kernel, scale),
        (f32(32, LANES), f32(GROUP, LANES)),
        *scores,
        received,
        row_joint,
        flops=2 * 1024 * 2048,
    )
    joint = call(core_kernel, f32(24, LANES), joint, move(joint, to_core))
    sent = call(join_kernel, f32(ZS * 24, LANES), joint, move(joint, to_far))
    along_z = [[2 * z + k for z in range(ZS)] for k in range(2)]
    received = lax.all_to_all(sent, "wide", 0, 0, axis_index_groups=along_z, tiled=True)
    sent, row_best = call(
        functools.partial(col_best_kernel, scale),
        (f32(GROUP, LANES), f32(8, LANES)),
        *scores,
        received,
        col_norm,
        flops=2 * 1024 * 2048,
    )
    received = exchange(sent)
    col_best = call(last_kernel, f32(1, LANES), received)
    return row_best.reshape(1024), col_best.reshape(LANES)


def solution(mesh):
    return jax.shard_map(
        body,
        mesh=mesh,
        in_specs=(P("narrow", None), P(("wide", "narrow"), None)),
        out_specs=(P("narrow"), P(("wide", "narrow"))),
        check_vma=False,
    )
```

```python
import functools
import math

import jax
import jax.numpy as jnp
from jax import lax
from jax.experimental import pallas as pl
from jax.experimental.pallas import tpu as pltpu
from jax.sharding import PartitionSpec as P

XS, YS, ZS, CORES = 4, 4, 8, 2
BOTH = ("wide", "narrow")
GROUP = 8
LANES = 128


def device_index(z, y, x, core):
    y, x, z = y % YS, x % XS, z % ZS
    return (z * 2 + y // 2) * 16 + (y % 2) * 8 + x * 2 + core


def places():
    for z in range(ZS):
        for y in range(YS):
            for x in range(XS):
                for core in range(CORES):
                    yield z, y, x, core


def partner(y, core):
    return y ^ 1 if core == 0 else 3 - y


def move(value, where):
    pairs = [(device_index(*place), device_index(*where(*place))) for place in places()]
    return lax.ppermute(value, BOTH, pairs)


def ahead(z, y, x, core):
    return z, y, x + 1 - 2 * core, core


def behind(z, y, x, core):
    return z, y, x - 1 + 2 * core, core


def across(z, y, x, core):
    return z, partner(y, core), x, core


def ahead_across(z, y, x, core):
    return z, partner(y, core), x + 1 - 2 * core, core


def to_core(z, y, x, core):
    return z, y, x, 1 - core


def to_far(z, y, x, core):
    return z, y + 2, x, core


def column_groups():
    groups = []
    for z in range(ZS):
        for core in range(CORES):
            for y in (0, 2):
                rows = (y, partner(y, core))
                groups.append([device_index(z, row, x, core) for row in rows for x in range(XS)])
    return groups


def vmem():
    return pl.BlockSpec(memory_space=pltpu.VMEM)


def after(values):
    return lax.optimization_barrier(values)


def held(value):
    return pltpu.with_memory_space_constraint(value, pltpu.VMEM)


def call(kernel, out_shape, *operands, flops=0, exps=0, scratch=(), far=(), limit=24):
    moved = sum(math.prod(o.shape) * o.dtype.itemsize for o in operands)
    return pl.pallas_call(
        kernel,
        out_shape=out_shape,
        in_specs=[pl.BlockSpec(memory_space=pltpu.HBM) if k in far else vmem() for k in range(len(operands))],
        out_specs=jax.tree.map(lambda _: vmem(), out_shape),
        scratch_shapes=list(scratch),
        cost_estimate=pl.CostEstimate(flops=flops, bytes_accessed=moved, transcendentals=exps),
        compiler_params=pltpu.CompilerParams(vmem_limit_bytes=limit * 1024 * 1024),
    )(*operands)


def f32(*shape):
    return jax.ShapeDtypeStruct(shape, jnp.float32)


def eye():
    row = lax.broadcasted_iota(jnp.int32, (LANES, LANES), 0)
    return row == lax.broadcasted_iota(jnp.int32, (LANES, LANES), 1)


def as_row(column):
    return jnp.sum(jnp.where(eye(), column, 0.0), axis=0, keepdims=True)


def as_column(row):
    return jnp.sum(jnp.where(eye(), row, 0.0), axis=1, keepdims=True)


def own_place():
    narrow = lax.axis_index("narrow")
    return narrow // 8, (narrow // 2) % 4, narrow % 2


def owner(place, slot):
    y_lo, x, core = place
    dx, dy = slot
    return ((y_lo + dy) % 2) * 4 + (x + 4 + dx * (1 - 2 * core)) % 4


CALLS = (((0, 0), (0, 1)), ((3, 0), (1, 0)), ((2, 1), (3, 1), (2, 0)), ((1, 1),))
SLOTS = tuple((call, k, slot) for call, slots in enumerate(CALLS) for k, slot in enumerate(slots))


def products(scale, s0, s1, targets, scores, row_part):
    count = targets.shape[0]
    rate = scale / math.log(2.0)
    running = None
    for i in range(8):
        source = (s0 if i < 4 else s1)[pl.ds((i % 4) * 256, 256), :]
        part = lax.dot_general(
            targets, source, (((1,), (1,)), ((), ())), preferred_element_type=jnp.float32
        )
        scores[:, pl.ds(i * 256, 256)] = part
        top = jnp.max(part, axis=0, keepdims=True)
        total = jnp.sum(jnp.exp2((part - top) * rate), axis=0, keepdims=True)
        result = top * scale + jnp.log(total)
        row_part[pl.ds(2 * i, 1), :] = result[:, :LANES]
        row_part[pl.ds(2 * i + 1, 1), :] = result[:, LANES:]
        top = jnp.maximum(part[:, :LANES], part[:, LANES:])
        running = top if running is None else jnp.maximum(running, top)
    top = jnp.max(running, axis=1, keepdims=True)
    total = jnp.zeros((count, LANES), jnp.float32)
    for j in range(16):
        total += jnp.exp2((scores[:, pl.ds(j * LANES, LANES)] - top) * rate)
    result = top * scale + jnp.log(jnp.sum(total, axis=1, keepdims=True))
    return [as_row(result[k : k + LANES]) for k in range(0, count, LANES)]


def bring_kernel(sources, targets, sources_here, targets_here, sems):
    copies = [pltpu.make_async_copy(targets, targets_here, sems.at[0])]
    for i in range(8):
        rows = pl.ds(i * 128, 128)
        copies.append(pltpu.make_async_copy(sources.at[rows], sources_here.at[rows], sems.at[i + 1]))
    for copy in copies:
        copy.start()
    for copy in copies:
        copy.wait()


def some_kernel(scale, s0, s1, *refs):
    blocks, (scores, row_part, col_part) = refs[:-3], refs[-3:]
    targets = jnp.concatenate([block[...] for block in blocks], axis=0)
    for k, row in enumerate(products(scale, s0, s1, targets, scores, row_part)):
        col_part[pl.ds(k, 1), :] = row


def end_kernel(scale, s0, s1, ta, *refs):
    rows, cols = refs[:3], refs[3:6]
    scores, joint, sent, scratch, last = refs[6:]
    ends = products(scale, s0, s1, ta[...], scores, last)
    joint[...] = log_sum([row[...] for row in rows] + [last[...]])
    place = own_place()
    for call, k, slot in SLOTS:
        row = ends[k] if call == 3 else cols[call][pl.ds(k, 1), :]
        scratch[pl.ds(owner(place, slot), 1), :] = row
    whole = scratch[...]
    for e in range(GROUP):
        sent[pl.ds(e * GROUP, GROUP), :] = whole


def log_sum(parts):
    top = functools.reduce(jnp.maximum, parts)
    return top + jnp.log(sum(jnp.exp(part - top) for part in parts))


def row_best_kernel(scale, a0, a1, a2, a3, received, row_joint, rows, col_norm):
    norm = log_sum([received[pl.ds(e * GROUP, GROUP), :] for e in range(GROUP)])
    col_norm[...] = norm
    place = own_place()
    half = 0.5 / scale
    best = [None] * 16
    for call, k, slot in SLOTS:
        column = as_column(col_norm[pl.ds(owner(place, slot), 1), :]) * half
        column = jnp.broadcast_to(column, (LANES, LANES))
        block = (a0, a1, a2, a3)[call]
        for j in range(16):
            part = block[pl.ds(k * LANES, LANES), pl.ds(j * LANES, LANES)] - column
            part = functools.reduce(jnp.maximum, [part[8 * q : 8 * q + 8] for q in range(16)])
            best[j] = part if best[j] is None else jnp.maximum(best[j], part)
    rows[:16] = row_joint[...]
    for j in range(16):
        rows[pl.ds(16 + j, 1), :] = jnp.max(best[j], axis=0, keepdims=True) * scale


def core_kernel(rows, core, joint):
    joint[:8] = log_sum([rows[:8], core[8:16]])
    joint[8:16] = log_sum([rows[8:16], core[:8]])
    joint[16:] = jnp.maximum(rows[16:24], core[24:])


def join_kernel(rows, far, sent):
    norm = log_sum([rows[:16], far[:16]])
    best = jnp.maximum(rows[16:], far[16:])
    for e in range(ZS):
        sent[pl.ds(e * 24, 16), :] = norm
        sent[pl.ds(e * 24 + 16, 8), :] = best


def col_best_kernel(scale, a0, a1, a2, a3, received, col_norm, sent, row_best):
    parts = [received[pl.ds(e * 24, 16), :] for e in range(ZS)]
    row_norm = log_sum(parts)
    best = functools.reduce(jnp.maximum, [received[pl.ds(e * 24 + 16, 8), :] for e in range(ZS)])
    row_best[...] = best - 0.5 * row_norm[:8]
    place = own_place()
    norms = row_norm * (0.5 / scale)
    for call, k, slot in SLOTS:
        block = (a0, a1, a2, a3)[call]
        best = None
        for j in range(16):
            part = block[pl.ds(k * LANES, LANES), pl.ds(j * LANES, LANES)] - norms[j : j + 1, :]
            best = part if best is None else jnp.maximum(best, part)
        best = as_row(jnp.max(best, axis=1, keepdims=True)) * scale
        position = owner(place, slot)
        sent[pl.ds(position, 1), :] = best - 0.5 * col_norm[pl.ds(position, 1), :]


def body(sources, targets):
    scale = 1.0 / math.sqrt(sources.shape[1])
    groups = column_groups()

    def exchange(value):
        return lax.all_to_all(value, BOTH, 0, 0, axis_index_groups=groups, tiled=True)

    def kept(rows):
        return pltpu.VMEM((rows, 2048), jnp.float32)

    blocks = {}
    blocks[3, 0] = move(targets, ahead)
    blocks[0, 1] = move(targets, across)
    other = held(move(sources, to_core))
    sources, blocks[0, 0] = call(
        bring_kernel,
        (pltpu.VMEM((1024, 1024), jnp.bfloat16), pltpu.VMEM((LANES, 1024), jnp.bfloat16)),
        pltpu.with_memory_space_constraint(sources, pltpu.HBM),
        pltpu.with_memory_space_constraint(targets, pltpu.HBM),
        far=(0, 1),
        scratch=[pltpu.SemaphoreType.DMA((9,))],
    )
    blocks[1, 0] = move(blocks[0, 0], behind)
    blocks[3, 0], blocks[0, 0] = after((blocks[3, 0], blocks[0, 0]))
    blocks[3, 1] = move(blocks[3, 0], across)
    blocks[2, 0] = move(blocks[3, 0], ahead)
    blocks[2, 1] = move(blocks[3, 0], ahead_across)
    both = (held(sources), other)

    scores, rows, cols = [], [], []
    for n, slots in enumerate(CALLS[:-1]):
        count = len(slots) * LANES
        if n == 1:
            blocks[1, 0], rows[0] = after((blocks[1, 0], rows[0]))
            blocks[1, 1] = move(blocks[1, 0], across)
        part, row, col = call(
            functools.partial(some_kernel, scale),
            (kept(count), f32(16, LANES), f32(len(slots), LANES)),
            *both,
            *[blocks[slot] for slot in slots],
            flops=2 * count * 2048 * 1024,
            exps=2 * count * 2048,
        )
        scores.append(held(part))
        rows.append(row)
        cols.append(col)
    part, row_joint, sent = call(
        functools.partial(end_kernel, scale),
        (kept(LANES), f32(16, LANES), f32(GROUP * GROUP, LANES)),
        *both,
        *[blocks[slot] for slot in CALLS[-1]],
        *rows,
        *cols,
        flops=2 * LANES * 2048 * 1024,
        exps=2 * LANES * 2048,
        scratch=[pltpu.VMEM((GROUP, LANES), jnp.float32), pltpu.VMEM((16, LANES), jnp.float32)],
    )
    scores.append(held(part))
    received = exchange(sent)
    joint, col_norm = call(
        functools.partial(row_best_kernel, scale),
        (f32(32, LANES), f32(GROUP, LANES)),
        *scores,
        received,
        row_joint,
        flops=2 * 1024 * 2048,
    )
    joint = call(core_kernel, f32(24, LANES), joint, move(joint, to_core))
    sent = call(join_kernel, f32(ZS * 24, LANES), joint, move(joint, to_far))
    along_z = [[2 * z + k for z in range(ZS)] for k in range(2)]
    received = lax.all_to_all(sent, "wide", 0, 0, axis_index_groups=along_z, tiled=True)
    sent, row_best = call(
        functools.partial(col_best_kernel, scale),
        (f32(GROUP, LANES), f32(8, LANES)),
        *scores,
        received,
        col_norm,
        flops=2 * 1024 * 2048,
    )
    received = exchange(sent)
    col_best = jnp.max(received, axis=0)
    return row_best.reshape(1024), col_best.reshape(LANES)


def solution(mesh):
    return jax.shard_map(
        body,
        mesh=mesh,
        in_specs=(P("narrow", None), P(("wide", "narrow"), None)),
        out_specs=(P("narrow"), P(("wide", "narrow"))),
        check_vma=False,
    )
```
